32 devices in a mesh: seq: 8 (over z, y), batch: 4 (over x, core).
Axes of the slice: x: 2, y: 2, z: 4, core: 2. Of those that a mesh axis runs over, the one named last changes fastest.
Arguments:
- tokens: bfloat16 [4, 1024, 1408], P('batch', 'seq')
- qkv_weight: bfloat16 [1408, 4224], P('batch'), may hold values from -0.15625 to 0.15625
- out_weight: bfloat16 [1408, 1408], P('batch'), may hold values from -0.15625 to 0.15625
- mask_blocks: int32 [4, 14], replicated, may hold values from 0 to 15, as said below
- owner_map: int32 [4, 16], replicated, may hold values from 0 to 3, as said below
- pred_stream: bfloat16 [4, 4, 1024, 384], P('batch', None, 'seq'), may hold values from -6 to 6
- pred_up: bfloat16 [384, 1536], replicated, may hold values from -0.3125 to 0.3125
- pred_down: bfloat16 [1536, 384], replicated, may hold values from -0.15625 to 0.15625
- pred_proj: bfloat16 [384, 1408], replicated, may hold values from -0.3125 to 0.3125
Outputs:
- grad_up: float32 [384, 1536], P(None, ('seq', 'batch'))
- grad_down: float32 [1536, 384], P(('seq', 'batch'))
The draws below stay inside these ranges and needn't reach their ends.
Inputs may be any that keep to these rules, and one draw needn't show every extreme that they name: `mask_blocks`: the 14 entries of one clip are distinct block indices; each aligned group of 2 blocks (those of one device) holds 2 or 1 of them. `owner_map`: within one clip, the blocks of one aligned group of 2 have distinct owners.
All inputs are finite; a program needn't handle non-finite values.
Results may differ from the reference program's by a relative error of at most 0.005.
Values may be sent and summed in bfloat16 or wider, within the bound.
No kernel may reach another device: no remote copies, remote signals or barrier semaphores. Data moves between devices by JAX's collectives and lax.ppermute only.
A program may use at most 128 MiB of HBM per device.

```python
import jax
import jax.numpy as jnp
from jax import lax

D = 1408
H = 16
HD = 88
PD = 384
PH = 1536
BLK = 64
BLK_DEV = 2
TOKENS = 1024
BLOCKS = 16
MASK_BLK = 14
BATCH = 4


pattern_count = 32


def joint_draw(key):
    base = jax.random.fold_in(key, 29)
    groups = BLOCKS // BLK_DEV
    key_star, key_owner, key_clips = jax.random.split(base, 3)
    star_group = jax.random.randint(key_star, (), 0, groups)
    star_owner = jax.random.randint(key_owner, (), 0, BATCH).astype(jnp.int32)
    position = jnp.arange(BLK_DEV, dtype=jnp.int32)

    def one_clip(clip_key):
        key_a, key_b, key_c, key_d = jax.random.split(clip_key, 4)
        order = jax.random.permutation(key_a, groups)
        single = jnp.zeros((groups,), jnp.int32).at[order[:groups // 4]].set(1)
        dropped = jax.random.randint(key_b, (groups,), 0, BLK_DEV)
        masked = 1 - single[:, None] * (position[None, :] == dropped[:, None]).astype(jnp.int32)
        owner_keys = jax.random.split(key_c, groups)
        rows = jax.vmap(lambda one_key: jax.random.permutation(one_key, BATCH)[:BLK_DEV])(owner_keys).astype(jnp.int32)
        first = jnp.where(masked[:, 0] == 1, 0, 1).astype(jnp.int32)
        at_first = jnp.take_along_axis(rows, first[:, None], axis=1)
        swapped = jnp.where(rows == star_owner, at_first, rows)
        forced = jnp.where(position[None, :] == first[:, None], star_owner, swapped)
        is_star = (jnp.arange(groups) == star_group)[:, None]
        owners = jnp.where(is_star, forced, rows).reshape(BLOCKS).astype(jnp.int32)
        flat_masked = masked.reshape(BLOCKS)
        ranks = jax.random.permutation(key_d, BLOCKS).astype(jnp.int32)
        score = jnp.where(flat_masked == 1, ranks, BLOCKS + jnp.arange(BLOCKS, dtype=jnp.int32))
        picked = jnp.argsort(score, stable=True)[:MASK_BLK].astype(jnp.int32)
        return (picked, owners)
    clip_keys = jax.random.split(key_clips, BATCH)
    return jax.vmap(one_clip)(clip_keys)


def draw_mask_blocks(key, part):
    return joint_draw(key)[0].astype(jnp.int32)


def draw_owner_map(key, part):
    return joint_draw(key)[1].astype(jnp.int32)


def draw_tokens(key, part):
    key_common, key_noise, key_assign = jax.random.split(jax.random.fold_in(key, 41), 3)
    common = jax.random.normal(key_common, (BATCH, pattern_count, D), jnp.float32)
    assign = jax.random.randint(key_assign, (BATCH, TOKENS), 0, pattern_count).astype(jnp.int32)
    spread = jax.vmap(lambda table, which: table[which])(common, assign)
    noise = jax.random.normal(key_noise, (BATCH, TOKENS, D), jnp.float32)
    scales = jnp.ones((BATCH, TOKENS, 1), jnp.float32)
    values = 0.1 * scales * (spread + 0.5 * noise)
    return values.astype(jnp.bfloat16)


def block_scale(stream_key, extent, cuts, smallest, largest):
    def one(dim, shards_of):
        steps = jax.random.uniform(jax.random.fold_in(jax.random.fold_in(stream_key, 6), dim), (shards_of,), jnp.float32, smallest / len(cuts), largest / len(cuts))
        return jnp.repeat(jnp.exp(steps), extent[dim] // shards_of).reshape((-1,) + (1,) * (len(extent) - dim - 1))

    level = one(*cuts[0])
    for cut in cuts[1:]:
        level = level * one(*cut)
    return level


def scatter_about(key, extent, scale, bound, pieces=(), kind=jnp.bfloat16):
    values = scale * jax.random.normal(key, extent, jnp.float32)
    if pieces:
        values = values * block_scale(key, extent, pieces, -0.22, 0.18)
    return jnp.clip(values, -bound, bound).astype(kind)


def setup_inputs(seed: int = 0) -> dict:
    key_list = jax.random.split(jax.random.key(seed), 10)
    return {
        "tokens": draw_tokens(jax.random.fold_in(key_list[9], 71), 0),
        "qkv_weight": scatter_about(key_list[1], (D, 3 * D), D ** -0.5, 0.15625, ((0, 4),)),
        "out_weight": scatter_about(key_list[2], (D, D), D ** -0.5, 0.15625, ((0, 4),)),
        "mask_blocks": draw_mask_blocks(jax.random.fold_in(key_list[9], 71), 0),
        "owner_map": draw_owner_map(jax.random.fold_in(key_list[9], 71), 0),
        "pred_stream": scatter_about(key_list[5], (BATCH, BATCH, TOKENS, PD), 1.0, 6.0, ((0, 4), (2, 8))),
        "pred_up": scatter_about(key_list[6], (PD, PH), PD ** -0.5, 0.3125),
        "pred_down": scatter_about(key_list[7], (PH, PD), PH ** -0.5, 0.15625),
        "pred_proj": scatter_about(key_list[8], (PD, D), PD ** -0.5, 0.3125),
    }


gelu_coef = 0.7978845608
gelu_cube = 0.044715

def layer_norm(values):
    center = values - lax.optimization_barrier(jnp.mean(values, axis=-1, keepdims=True))
    variance = lax.optimization_barrier(jnp.mean(center * center, axis=-1, keepdims=True))
    factor = lax.rsqrt(variance + 1e-06)
    return (center * factor, factor)

def gelu_tanh(values):
    inner = gelu_coef * (values + gelu_cube * values * values * values)
    return 0.5 * values * (1.0 + jnp.tanh(inner))

def gelu_slope(values):
    inner = gelu_coef * (values + gelu_cube * values * values * values)
    tangent = jnp.tanh(inner)
    return 0.5 * (1.0 + tangent) + 0.5 * values * (1.0 - tangent * tangent) * gelu_coef * (1.0 + 3.0 * gelu_cube * values * values)

def predictor_grads(stream, target_rows, live_rows, pred_up, pred_down, pred_proj, divisor):
    stream_f = stream.astype(jnp.float32)
    normed_pred = layer_norm(stream_f)[0].astype(jnp.bfloat16)
    hidden_pre = jnp.dot(normed_pred, pred_up, preferred_element_type=jnp.float32)
    hidden = gelu_tanh(hidden_pre).astype(jnp.bfloat16)
    mixed = stream_f + jnp.dot(hidden, pred_down, preferred_element_type=jnp.float32)
    mixed_norm, rstd = layer_norm(mixed)
    mixed_rounded = mixed_norm.astype(jnp.bfloat16)
    prediction = jnp.dot(mixed_rounded, pred_proj, preferred_element_type=jnp.float32)
    error = (prediction - target_rows.astype(jnp.float32)) * live_rows[:, None]
    grad_pred = (error / divisor).astype(jnp.bfloat16)
    grad_norm = jnp.dot(grad_pred, pred_proj.T, preferred_element_type=jnp.float32)
    first_mean = lax.optimization_barrier(jnp.mean(grad_norm, axis=-1, keepdims=True))
    second_mean = lax.optimization_barrier(jnp.mean(grad_norm * mixed_norm, axis=-1, keepdims=True))
    grad_mixed = (rstd * (grad_norm - first_mean - mixed_norm * second_mean)).astype(jnp.bfloat16)
    grad_down = jnp.dot(hidden.T, grad_mixed, preferred_element_type=jnp.float32)
    grad_hidden = jnp.dot(grad_mixed, pred_down.T, preferred_element_type=jnp.float32)
    grad_pre = (grad_hidden * gelu_slope(hidden_pre)).astype(jnp.bfloat16)
    grad_up = jnp.dot(normed_pred.T, grad_pre, preferred_element_type=jnp.float32)
    return (grad_up, grad_down)

def encode(clip_tokens, qkv_weight, out_weight):
    stream_f = clip_tokens.astype(jnp.float32)
    normed = layer_norm(stream_f)[0].astype(jnp.bfloat16)
    projected = jnp.dot(normed, qkv_weight, preferred_element_type=jnp.float32).astype(jnp.bfloat16)
    queries = projected[:, :D].reshape(TOKENS, H, HD).transpose(1, 0, 2)
    keys = projected[:, D:2 * D].reshape(TOKENS, H, HD).transpose(1, 0, 2)
    values = projected[:, 2 * D:].reshape(TOKENS, H, HD).transpose(1, 0, 2)
    scale = 1.0 / HD ** 0.5

    def one_head(inputs):
        head_q, head_k, head_v = inputs
        scores = jnp.dot(head_q, head_k.T, preferred_element_type=jnp.float32) * scale
        weights = jnp.exp(scores)
        totals = lax.optimization_barrier(jnp.sum(weights, axis=1))
        summed = jnp.dot(weights.astype(jnp.bfloat16), head_v, preferred_element_type=jnp.float32)
        return summed / totals[:, None]
    heads_out = lax.map(one_head, (queries, keys, values))
    attended = heads_out.transpose(1, 0, 2).reshape(TOKENS, D).astype(jnp.bfloat16)
    summed = stream_f + jnp.dot(attended, out_weight, preferred_element_type=jnp.float32)
    return layer_norm(summed)[0].astype(jnp.bfloat16)

def reference(tokens, qkv_weight, out_weight, mask_blocks, owner_map, pred_stream, pred_up, pred_down, pred_proj):
    target = lax.map(lambda clip_tokens: encode(clip_tokens, qkv_weight, out_weight), tokens)
    block_index = jnp.arange(BLOCKS, dtype=jnp.int32)
    masked = jnp.any(mask_blocks[:, :, None] == block_index[None, None, :], axis=1)
    token_block = jnp.arange(TOKENS, dtype=jnp.int32) // BLK
    live_tok = masked[:, token_block].astype(jnp.float32)
    owner_tok = owner_map[:, token_block].astype(jnp.int32)
    picked = jnp.take_along_axis(pred_stream, owner_tok[None, :, :, None], axis=0)[0]
    divisor = float(BATCH * MASK_BLK)
    return predictor_grads(picked.reshape(BATCH * TOKENS, PD), target.reshape(BATCH * TOKENS, D), live_tok.reshape(BATCH * TOKENS), pred_up, pred_down, pred_proj, divisor)
```

```python
import jax
import jax.numpy as jnp
from jax import lax
from jax.experimental import pallas as pl
from jax.experimental.pallas import tpu as pltpu
from jax.sharding import PartitionSpec as P

H = 16
HD = 88
BLK = 64


gelu_coef = 0.7978845608
gelu_cube = 0.044715


def layer_norm(values):
    center = values - jnp.mean(values, axis=-1, keepdims=True)
    variance = jnp.mean(center * center, axis=-1, keepdims=True)
    factor = lax.rsqrt(variance + 1e-06)
    return (center * factor, factor)


def gelu_tanh(values):
    inner = gelu_coef * (values + gelu_cube * values * values * values)
    return 0.5 * values * (1.0 + jnp.tanh(inner))


def gelu_slope(values):
    inner = gelu_coef * (values + gelu_cube * values * values * values)
    tangent = jnp.tanh(inner)
    return 0.5 * (1.0 + tangent) + 0.5 * values * (1.0 - tangent * tangent) * gelu_coef * (
        1.0 + 3.0 * gelu_cube * values * values
    )


def predictor_grads(stream, target_rows, live_rows, pred_up, pred_down, pred_proj, divisor):
    stream_f = stream.astype(jnp.float32)
    normed_pred = layer_norm(stream_f)[0].astype(jnp.bfloat16)
    hidden_pre = jnp.dot(normed_pred, pred_up, preferred_element_type=jnp.float32)
    hidden = gelu_tanh(hidden_pre).astype(jnp.bfloat16)
    mixed = stream_f + jnp.dot(hidden, pred_down, preferred_element_type=jnp.float32)
    mixed_norm, rstd = layer_norm(mixed)
    mixed_rounded = mixed_norm.astype(jnp.bfloat16)
    prediction = jnp.dot(mixed_rounded, pred_proj, preferred_element_type=jnp.float32)
    error = (prediction - target_rows.astype(jnp.float32)) * live_rows[:, None]
    grad_pred = (error / divisor).astype(jnp.bfloat16)
    grad_norm = jnp.dot(grad_pred, pred_proj.T, preferred_element_type=jnp.float32)
    first_mean = jnp.mean(grad_norm, axis=-1, keepdims=True)
    second_mean = jnp.mean(grad_norm * mixed_norm, axis=-1, keepdims=True)
    grad_mixed = (rstd * (grad_norm - first_mean - mixed_norm * second_mean)).astype(jnp.bfloat16)
    grad_down = jnp.dot(hidden.T, grad_mixed, preferred_element_type=jnp.float32)
    grad_hidden = jnp.dot(grad_mixed, pred_down.T, preferred_element_type=jnp.float32)
    grad_pre = (grad_hidden * gelu_slope(hidden_pre)).astype(jnp.bfloat16)
    grad_up = jnp.dot(normed_pred.T, grad_pre, preferred_element_type=jnp.float32)
    return (grad_up, grad_down)


def per_device(
    tokens,
    qkv_weight,
    out_weight,
    mask_blocks,
    owner_map,
    pred_stream,
    pred_up,
    pred_down,
    pred_proj,
):
    stream_in = tokens[0]
    tok_rows, width = stream_in.shape
    clip_now = lax.axis_index("batch")
    shard_now = lax.axis_index("seq")
    owners = lax.axis_size("batch")
    stream_f = stream_in.astype(jnp.float32)
    normed = layer_norm(stream_f)[0].astype(jnp.bfloat16)

    def fold_rows(left, piece):
        return jnp.dot(left, piece, preferred_element_type=jnp.float32)

    projected = fold_rows(normed, lax.all_gather(qkv_weight, "batch", axis=0, tiled=True))
    projected = projected.astype(jnp.bfloat16)
    queries = projected[:, :width].reshape(tok_rows, H, HD)
    keys_values = projected[:, width:]
    scale = 1.0 / HD**0.5

    def attend_block(carry, block):
        weighted, totals = carry
        block_keys = block[:, :width].reshape(block.shape[0], H, HD)
        block_values = block[:, width:].reshape(block.shape[0], H, HD)
        scores = (
            jnp.einsum("qhd,khd->hqk", queries, block_keys, preferred_element_type=jnp.float32)
            * scale
        )
        weights = jnp.exp(scores)
        totals = totals + jnp.sum(weights, axis=2)
        weighted = weighted + jnp.einsum(
            "hqk,khd->qhd",
            weights.astype(jnp.bfloat16),
            block_values,
            preferred_element_type=jnp.float32,
        )
        return (weighted, totals)

    start_state = (jnp.zeros((tok_rows, H, HD), jnp.float32), jnp.zeros((H, tok_rows), jnp.float32))
    piece = lax.all_gather(keys_values, "seq", axis=0, tiled=True)
    rows = piece.shape[0]
    blocks = piece.reshape(rows // 512, 512, piece.shape[1])
    weighted, totals = lax.scan(
        lambda state, block: (attend_block(state, block), None), start_state, blocks
    )[0]
    attended = (weighted / totals.T[:, :, None]).reshape(tok_rows, width).astype(jnp.bfloat16)
    attn_out = fold_rows(attended, lax.all_gather(out_weight, "batch", axis=0, tiled=True))
    target = layer_norm(stream_f + attn_out)[0].astype(jnp.bfloat16)
    blocks_dev = tok_rows // BLK
    block_ids = shard_now * blocks_dev + jnp.arange(blocks_dev, dtype=jnp.int32)
    owner_ids = jnp.arange(owners, dtype=jnp.int32)
    all_masked = jnp.any(mask_blocks[:, :, None] == block_ids[None, None, :], axis=1)
    all_owner = lax.dynamic_slice_in_dim(owner_map, shard_now * blocks_dev, blocks_dev, 1)
    my_masked = lax.dynamic_slice_in_dim(all_masked, clip_now, 1, 0)[0]
    my_owner = lax.dynamic_slice_in_dim(all_owner, clip_now, 1, 0)[0]
    send_select = (my_masked[None, :] & (my_owner[None, :] == owner_ids[:, None])).astype(
        jnp.bfloat16
    )
    target_blocks = target.reshape(blocks_dev, BLK, width)
    outgoing = jnp.einsum(
        "ob,brd->ord", send_select, target_blocks, preferred_element_type=jnp.float32
    ).astype(jnp.bfloat16)
    incoming = lax.all_to_all(outgoing, "batch", split_axis=0, concat_axis=0, tiled=True)
    recv_flags = all_masked & (all_owner == clip_now)
    recv_select = recv_flags.astype(jnp.bfloat16)
    live_clip = jnp.any(recv_flags, axis=1).astype(jnp.float32)
    live_rows = jnp.broadcast_to(live_clip[:, None], (owners, BLK)).reshape(owners * BLK)
    stream_blocks = pred_stream[0].reshape(owners, blocks_dev, BLK, pred_stream.shape[3])
    stream_picked = jnp.einsum(
        "cb,cbrd->crd", recv_select, stream_blocks, preferred_element_type=jnp.float32
    ).astype(jnp.bfloat16)
    stream_rows = stream_picked.reshape(owners * BLK, pred_stream.shape[3])
    target_rows = incoming.reshape(owners * BLK, width)
    divisor = float(owners * mask_blocks.shape[1])
    grad_up, grad_down = predictor_grads(
        stream_rows, target_rows, live_rows, pred_up, pred_down, pred_proj, divisor
    )
    return (
        lax.psum_scatter(grad_up, ("seq", "batch"), scatter_dimension=1, tiled=True),
        lax.psum_scatter(grad_down, ("seq", "batch"), scatter_dimension=0, tiled=True),
    )


def take(array, index):
    return lax.dynamic_index_in_dim(array, index, 0, keepdims=False)


def weight_kernel(place_ref, own_ref, one_ref, two_ref, three_ref, out_ref, held):
    place = place_ref[0]
    for step, piece_ref in enumerate((own_ref, one_ref, two_ref, three_ref)):
        held[place ^ step] = piece_ref[...]
    slabs, rows, columns = held.shape
    out_ref[...] = held[...].reshape(slabs * rows, columns).T


def attend_kernel(normed_ref, weight_ref, out_ref, projected):
    projected[...] = lax.dot_general(
        weight_ref[...],
        normed_ref[...],
        (((1,), (1,)), ((), ())),
        preferred_element_type=jnp.float32,
    )
    part = projected.shape[0] // 3
    blocks, _, block_rows = out_ref.shape
    pad = jnp.zeros((-HD % 128, projected.shape[1]), jnp.float32)
    log2_scale = 1.4426950408889634 / HD**0.5

    def head_rows(which, head):
        start = which * part + head * HD
        rows = projected[start : start + HD, :]
        return jnp.concatenate([rows, pad], axis=0).astype(jnp.bfloat16)

    wide = 2
    for head in range(part // HD):
        queries = head_rows(0, head)
        keys = head_rows(1, head).T
        values = head_rows(2, head)
        for block in range(blocks // wide):
            span = block_rows * wide
            scores = jnp.dot(
                keys,
                queries[:, block * span : (block + 1) * span],
                preferred_element_type=jnp.float32,
            )
            weights = jnp.exp2(scores * log2_scale)
            totals = jnp.sum(weights, axis=0, keepdims=True)
            summed = jnp.dot(
                values, weights.astype(jnp.bfloat16), preferred_element_type=jnp.float32
            )
            attended = summed[:HD] / totals
            for inner in range(wide):
                out_ref[block * wide + inner, head * HD : (head + 1) * HD, :] = attended[
                    :, inner * block_rows : (inner + 1) * block_rows
                ]


def loss_kernel(
    place_ref,
    att_ref,
    own_ref,
    one_ref,
    two_ref,
    three_ref,
    raw_ref,
    prediction_ref,
    mixed_norm_ref,
    rstd_ref,
    live_ref,
    proj_ref,
    out_ref,
):
    place = place_ref[0]
    summed = raw_ref[...].astype(jnp.float32)
    for step, slab_ref in enumerate((own_ref, one_ref, two_ref, three_ref)):
        summed = summed + lax.dot_general(
            att_ref[place ^ step],
            slab_ref[...],
            (((0,), (0,)), ((), ())),
            preferred_element_type=jnp.float32,
        )
    target = layer_norm(summed)[0].astype(jnp.bfloat16)
    error = (prediction_ref[...] - target.astype(jnp.float32)) * live_ref[...]
    grad_pred = error.astype(jnp.bfloat16)
    grad_norm = lax.dot_general(
        grad_pred, proj_ref[...], (((1,), (1,)), ((), ())), preferred_element_type=jnp.float32
    )
    mixed_norm = mixed_norm_ref[...]
    first_mean = jnp.mean(grad_norm, axis=-1, keepdims=True)
    second_mean = jnp.mean(grad_norm * mixed_norm, axis=-1, keepdims=True)
    out_ref[...] = (rstd_ref[...] * (grad_norm - first_mean - mixed_norm * second_mean)).astype(
        jnp.bfloat16
    )


def grads_kernel(grad_ref, normed_ref, hidden_ref, slope_ref, down_ref, out_ref):
    grad_mixed = grad_ref[...]
    pieces, half, _ = out_ref.shape
    half = half // 2
    over_rows = (((0,), (0,)), ((), ()))
    grad_down = lax.dot_general(
        hidden_ref[...], grad_mixed, over_rows, preferred_element_type=jnp.float32
    )
    grad_hidden = lax.dot_general(
        grad_mixed, down_ref[...], (((1,), (1,)), ((), ())), preferred_element_type=jnp.float32
    )
    grad_pre = (grad_hidden * slope_ref[...]).astype(jnp.bfloat16)
    grad_up = lax.dot_general(
        grad_pre, normed_ref[...], over_rows, preferred_element_type=jnp.float32
    )
    for piece in range(pieces):
        rows = slice(piece * half, (piece + 1) * half)
        out_ref[piece, :half, :] = grad_up[rows].astype(jnp.bfloat16)
        out_ref[piece, half:, :] = grad_down[rows].astype(jnp.bfloat16)


def in_vmem(kernel, out_shape, operands, places=0, scratch=()):
    return pl.pallas_call(
        kernel,
        out_shape=out_shape,
        in_specs=[pl.BlockSpec(memory_space=pltpu.SMEM)] * places
        + [pl.BlockSpec(memory_space=pltpu.VMEM)] * (len(operands) - places),
        out_specs=pl.BlockSpec(memory_space=pltpu.VMEM),
        scratch_shapes=list(scratch),
        compiler_params=pltpu.CompilerParams(vmem_limit_bytes=40 * 2**20),
    )(*operands)


CLIP_GROUP = ("k", "zl", "y")
ROW_GROUP = ("y", "x", "k")
BATCH_GROUP = ("x", "k")
SUM_GROUP = ("zh", "zl")


def head_shard(
    tokens,
    qkv_weight,
    out_weight,
    mask_blocks,
    owner_map,
    pred_stream,
    pred_up,
    pred_down,
    pred_proj,
):
    zh, zl, y, x, k = (lax.axis_index(name) for name in ("zh", "zl", "y", "x", "k"))
    batch = 2 * x + k
    seq = 4 * zh + 2 * zl + y
    place = batch.astype(jnp.int32)[None]
    _, tok_rows, width = tokens.shape
    owners, blk_dev = pred_stream.shape[1], tok_rows // BLK
    pred_width, units = pred_up.shape

    def swap_clips(value):
        return lax.ppermute(value, ("zh", "k"), ((0, 0), (1, 2), (2, 1), (3, 3)))

    def swap(value, bits):
        return lax.ppermute(value, BATCH_GROUP, tuple((i, i ^ bits) for i in range(owners)))

    raw = swap_clips(tokens[0])

    part = width // 8

    def columns_of(core):
        first = (4 * core + 2 * zl + y) * part
        return jnp.concatenate(
            [
                lax.dynamic_slice(
                    qkv_weight, (0, which * width + first), (qkv_weight.shape[0], part)
                )
                for which in range(3)
            ],
            axis=1,
        )

    own_columns, other_columns = columns_of(k), columns_of(1 - k)
    qkv_two = swap(own_columns, 2)
    qkv_three = swap(other_columns, 3)
    qkv_one = swap(other_columns, 1)

    stream_blocks = pred_stream[0].reshape(owners, blk_dev, BLK, pred_width)
    owner_here = lax.dynamic_slice_in_dim(owner_map, seq * blk_dev, blk_dev, 1)
    mine = (owner_here == batch)[:, :, None, None]
    compact = jnp.sum(jnp.where(mine, stream_blocks, 0), axis=1).astype(jnp.bfloat16)
    arrived = lax.all_to_all(compact, BATCH_GROUP, split_axis=0, concat_axis=0, tiled=True)
    stream = jnp.concatenate(
        [take(arrived, take(owner_here, batch)[i]) for i in range(blk_dev)], axis=0
    )
    stream = swap_clips(stream)

    stream_f = stream.astype(jnp.float32)
    normed_pred = layer_norm(stream_f)[0].astype(jnp.bfloat16)
    normed_rows = lax.all_gather(normed_pred, ROW_GROUP, axis=0, tiled=True)

    raw_f = raw.astype(jnp.float32)
    normed = layer_norm(raw_f)[0].astype(jnp.bfloat16)
    normed_all = lax.all_gather(normed, CLIP_GROUP, axis=0, tiled=True)

    out_two = swap(out_weight, 2)
    out_one = swap(out_weight, 1)
    out_three = swap(out_two, 1)

    hidden = gelu_tanh(jnp.dot(normed_pred, pred_up, preferred_element_type=jnp.float32))
    mixed = stream_f + jnp.dot(
        hidden.astype(jnp.bfloat16), pred_down, preferred_element_type=jnp.float32
    )
    mixed_norm, rstd = layer_norm(mixed)
    prediction = jnp.dot(
        mixed_norm.astype(jnp.bfloat16), pred_proj, preferred_element_type=jnp.float32
    )

    mine_rows = 4 * y + batch
    up_mine = lax.dynamic_index_in_dim(
        pred_up.reshape(pred_width, 4, 8, units // 32), mine_rows, 2, keepdims=False
    ).reshape(pred_width, units // 8)
    down_mine = lax.dynamic_index_in_dim(
        pred_down.reshape(4, 8, units // 32, pred_width), mine_rows, 1, keepdims=False
    ).reshape(units // 8, pred_width)
    pre_rows = jnp.dot(normed_rows, up_mine, preferred_element_type=jnp.float32)
    hidden_rows = gelu_tanh(pre_rows).astype(jnp.bfloat16)
    slope_rows = gelu_slope(pre_rows)

    clip = 2 * x + zh
    shard = 4 * k + 2 * zl + y
    block_ids = shard * blk_dev + jnp.arange(blk_dev, dtype=jnp.int32)
    masked = jnp.any(take(mask_blocks, clip)[:, None] == block_ids[None, :], axis=0)
    divisor = float(owners * mask_blocks.shape[1])
    live = jnp.repeat(masked.astype(jnp.float32) / divisor, BLK)[:, None]

    slab = qkv_weight.shape[0]
    qkv_columns = in_vmem(
        weight_kernel,
        jax.ShapeDtypeStruct((3 * part, width), jnp.bfloat16),
        (place, own_columns, qkv_one, qkv_two, qkv_three),
        places=1,
        scratch=(pltpu.VMEM((owners, slab, 3 * part), jnp.bfloat16),),
    )
    attended = in_vmem(
        attend_kernel,
        jax.ShapeDtypeStruct((8, part, tok_rows), jnp.float32),
        (normed_all, qkv_columns),
        scratch=(pltpu.VMEM((3 * part, normed_all.shape[0]), jnp.float32),),
    ).astype(jnp.bfloat16)
    attended = lax.all_to_all(attended, CLIP_GROUP, split_axis=0, concat_axis=0, tiled=True)
    attended = attended.reshape(owners, slab, tok_rows)

    grad_mixed = in_vmem(
        loss_kernel,
        jax.ShapeDtypeStruct((tok_rows, pred_width), jnp.bfloat16),
        (
            place,
            attended,
            out_weight,
            out_one,
            out_two,
            out_three,
            raw,
            prediction,
            mixed_norm,
            rstd,
            live,
            pred_proj,
        ),
        places=1,
    )
    grad_rows = lax.all_gather(grad_mixed, ROW_GROUP, axis=0, tiled=True)
    grads = in_vmem(
        grads_kernel,
        jax.ShapeDtypeStruct((4, units // 16, pred_width), jnp.bfloat16),
        (grad_rows, normed_rows, hidden_rows, slope_rows, down_mine),
    )
    grads = lax.all_to_all(grads, SUM_GROUP, split_axis=0, concat_axis=0, tiled=True)
    total = jnp.sum(grads.astype(jnp.float32), axis=0)
    half = units // 32
    return total[:half].T, total[half:]


def solution(mesh):
    if mesh.shape["seq"] == 8 and mesh.shape["batch"] == 4:
        names = ("zh", "zl", "y", "x", "k")
        step, batch, seq = head_shard, BATCH_GROUP, names[:3]
        mesh = jax.sharding.Mesh(mesh.devices.reshape(2, 2, 2, 2, 2), names)
    else:
        step, batch, seq = per_device, "batch", "seq"
    everyone = (seq, batch) if isinstance(seq, str) else seq + batch
    in_specs = (
        P(batch, seq, None),
        P(batch, None),
        P(batch, None),
        P(),
        P(),
        P(batch, None, seq, None),
        P(),
        P(),
        P(),
    )
    out_specs = (P(None, everyone), P(everyone, None))
    return jax.shard_map(step, mesh=mesh, in_specs=in_specs, out_specs=out_specs, check_vma=False)
```

```python
import functools
import jax
import jax.numpy as jnp
from jax import lax
from jax.experimental import pallas as pl
from jax.experimental.pallas import tpu as pltpu
from jax.sharding import PartitionSpec as P

H = 16
HD = 88
BLK = 64


gelu_coef = 0.7978845608
gelu_cube = 0.044715


def layer_norm(values):
    center = values - jnp.mean(values, axis=-1, keepdims=True)
    variance = jnp.mean(center * center, axis=-1, keepdims=True)
    factor = lax.rsqrt(variance + 1e-06)
    return (center * factor, factor)


def gelu_tanh(values):
    inner = gelu_coef * (values + gelu_cube * values * values * values)
    return 0.5 * values * (1.0 + jnp.tanh(inner))


def gelu_slope(values):
    inner = gelu_coef * (values + gelu_cube * values * values * values)
    tangent = jnp.tanh(inner)
    return 0.5 * (1.0 + tangent) + 0.5 * values * (1.0 - tangent * tangent) * gelu_coef * (
        1.0 + 3.0 * gelu_cube * values * values
    )


def predictor_grads(stream, target_rows, live_rows, pred_up, pred_down, pred_proj, divisor):
    stream_f = stream.astype(jnp.float32)
    normed_pred = layer_norm(stream_f)[0].astype(jnp.bfloat16)
    hidden_pre = jnp.dot(normed_pred, pred_up, preferred_element_type=jnp.float32)
    hidden = gelu_tanh(hidden_pre).astype(jnp.bfloat16)
    mixed = stream_f + jnp.dot(hidden, pred_down, preferred_element_type=jnp.float32)
    mixed_norm, rstd = layer_norm(mixed)
    mixed_rounded = mixed_norm.astype(jnp.bfloat16)
    prediction = jnp.dot(mixed_rounded, pred_proj, preferred_element_type=jnp.float32)
    error = (prediction - target_rows.astype(jnp.float32)) * live_rows[:, None]
    grad_pred = (error / divisor).astype(jnp.bfloat16)
    grad_norm = jnp.dot(grad_pred, pred_proj.T, preferred_element_type=jnp.float32)
    first_mean = jnp.mean(grad_norm, axis=-1, keepdims=True)
    second_mean = jnp.mean(grad_norm * mixed_norm, axis=-1, keepdims=True)
    grad_mixed = (rstd * (grad_norm - first_mean - mixed_norm * second_mean)).astype(jnp.bfloat16)
    grad_down = jnp.dot(hidden.T, grad_mixed, preferred_element_type=jnp.float32)
    grad_hidden = jnp.dot(grad_mixed, pred_down.T, preferred_element_type=jnp.float32)
    grad_pre = (grad_hidden * gelu_slope(hidden_pre)).astype(jnp.bfloat16)
    grad_up = jnp.dot(normed_pred.T, grad_pre, preferred_element_type=jnp.float32)
    return (grad_up, grad_down)


def per_device(
    tokens,
    qkv_weight,
    out_weight,
    mask_blocks,
    owner_map,
    pred_stream,
    pred_up,
    pred_down,
    pred_proj,
):
    stream_in = tokens[0]
    tok_rows, width = stream_in.shape
    clip_now = lax.axis_index("batch")
    shard_now = lax.axis_index("seq")
    owners = lax.axis_size("batch")
    stream_f = stream_in.astype(jnp.float32)
    normed = layer_norm(stream_f)[0].astype(jnp.bfloat16)

    def fold_rows(left, piece):
        return jnp.dot(left, piece, preferred_element_type=jnp.float32)

    projected = fold_rows(normed, lax.all_gather(qkv_weight, "batch", axis=0, tiled=True))
    projected = projected.astype(jnp.bfloat16)
    queries = projected[:, :width].reshape(tok_rows, H, HD)
    keys_values = projected[:, width:]
    scale = 1.0 / HD**0.5

    def attend_block(carry, block):
        weighted, totals = carry
        block_keys = block[:, :width].reshape(block.shape[0], H, HD)
        block_values = block[:, width:].reshape(block.shape[0], H, HD)
        scores = (
            jnp.einsum("qhd,khd->hqk", queries, block_keys, preferred_element_type=jnp.float32)
            * scale
        )
        weights = jnp.exp(scores)
        totals = totals + jnp.sum(weights, axis=2)
        weighted = weighted + jnp.einsum(
            "hqk,khd->qhd",
            weights.astype(jnp.bfloat16),
            block_values,
            preferred_element_type=jnp.float32,
        )
        return (weighted, totals)

    start_state = (jnp.zeros((tok_rows, H, HD), jnp.float32), jnp.zeros((H, tok_rows), jnp.float32))
    piece = lax.all_gather(keys_values, "seq", axis=0, tiled=True)
    rows = piece.shape[0]
    blocks = piece.reshape(rows // 512, 512, piece.shape[1])
    weighted, totals = lax.scan(
        lambda state, block: (attend_block(state, block), None), start_state, blocks
    )[0]
    attended = (weighted / totals.T[:, :, None]).reshape(tok_rows, width).astype(jnp.bfloat16)
    attn_out = fold_rows(attended, lax.all_gather(out_weight, "batch", axis=0, tiled=True))
    target = layer_norm(stream_f + attn_out)[0].astype(jnp.bfloat16)
    blocks_dev = tok_rows // BLK
    block_ids = shard_now * blocks_dev + jnp.arange(blocks_dev, dtype=jnp.int32)
    owner_ids = jnp.arange(owners, dtype=jnp.int32)
    all_masked = jnp.any(mask_blocks[:, :, None] == block_ids[None, None, :], axis=1)
    all_owner = lax.dynamic_slice_in_dim(owner_map, shard_now * blocks_dev, blocks_dev, 1)
    my_masked = lax.dynamic_slice_in_dim(all_masked, clip_now, 1, 0)[0]
    my_owner = lax.dynamic_slice_in_dim(all_owner, clip_now, 1, 0)[0]
    send_select = (my_masked[None, :] & (my_owner[None, :] == owner_ids[:, None])).astype(
        jnp.bfloat16
    )
    target_blocks = target.reshape(blocks_dev, BLK, width)
    outgoing = jnp.einsum(
        "ob,brd->ord", send_select, target_blocks, preferred_element_type=jnp.float32
    ).astype(jnp.bfloat16)
    incoming = lax.all_to_all(outgoing, "batch", split_axis=0, concat_axis=0, tiled=True)
    recv_flags = all_masked & (all_owner == clip_now)
    recv_select = recv_flags.astype(jnp.bfloat16)
    live_clip = jnp.any(recv_flags, axis=1).astype(jnp.float32)
    live_rows = jnp.broadcast_to(live_clip[:, None], (owners, BLK)).reshape(owners * BLK)
    stream_blocks = pred_stream[0].reshape(owners, blocks_dev, BLK, pred_stream.shape[3])
    stream_picked = jnp.einsum(
        "cb,cbrd->crd", recv_select, stream_blocks, preferred_element_type=jnp.float32
    ).astype(jnp.bfloat16)
    stream_rows = stream_picked.reshape(owners * BLK, pred_stream.shape[3])
    target_rows = incoming.reshape(owners * BLK, width)
    divisor = float(owners * mask_blocks.shape[1])
    grad_up, grad_down = predictor_grads(
        stream_rows, target_rows, live_rows, pred_up, pred_down, pred_proj, divisor
    )
    return (
        lax.psum_scatter(grad_up, ("seq", "batch"), scatter_dimension=1, tiled=True),
        lax.psum_scatter(grad_down, ("seq", "batch"), scatter_dimension=0, tiled=True),
    )


def after(value, other):
    return lax.optimization_barrier((value, other))[0]


def take(array, index):
    return lax.dynamic_index_in_dim(array, index, 0, keepdims=False)


def start_copies(pairs, sems):
    copies = [pltpu.make_async_copy(*pair, sems.at[i]) for i, pair in enumerate(pairs)]
    for copy in copies:
        copy.start()
    return copies


def weight_kernel(place_ref, core_ref, *refs):
    *piece_refs, out_ref, held, turned = refs
    place, core = place_ref[0], core_ref[0]
    parts, slabs, rows, columns = held.shape
    part = out_ref.shape[0] // parts
    for step in range(slabs):
        held[:, place ^ step] = piece_refs[step][...]
    for which in range(parts):
        turned[...] = held[which].reshape(slabs * rows, columns).T
        start = pl.multiple_of(core * part, part)
        out_ref[which * part : (which + 1) * part, :] = turned[pl.ds(start, part), :]


def attend_kernel(weight_ref, normed_ref, out_ref, projected):
    projected[...] = lax.dot_general(
        weight_ref[...],
        normed_ref[...],
        (((1,), (1,)), ((), ())),
        preferred_element_type=jnp.float32,
    )
    part = projected.shape[0] // 3
    chips, cores, _, block_rows = out_ref.shape
    pad = jnp.zeros((-HD % 128, projected.shape[1]), jnp.float32)
    log2_scale = 1.4426950408889634 / HD**0.5

    def head_rows(which, head):
        start = which * part + head * HD
        rows = projected[start : start + HD, :]
        return jnp.concatenate([rows, pad], axis=0).astype(jnp.bfloat16)

    heads = part // HD
    operands = [(head_rows(0, h), head_rows(1, h).T, head_rows(2, h)) for h in range(heads)]
    span = block_rows * cores
    for chip in range(chips):
        joined = []
        for queries, keys, values in operands:
            scores = jnp.dot(
                keys,
                queries[:, chip * span : (chip + 1) * span],
                preferred_element_type=jnp.float32,
            )
            weights = jnp.exp2(scores * log2_scale)
            totals = jnp.sum(weights, axis=0, keepdims=True)
            summed = jnp.dot(
                values, weights.astype(jnp.bfloat16), preferred_element_type=jnp.float32
            )
            joined.append(summed[:HD] / totals)
        attended = jnp.concatenate(joined, axis=0).astype(jnp.bfloat16)
        for core in range(cores):
            out_ref[chip, core] = attended[:, core * block_rows : (core + 1) * block_rows]


def partial_kernel(
    x_ref, core_ref, own_ref, two_ref, att_ref, keep_ref, give_ref, slabs, sems
):
    x, core = x_ref[0], core_ref[0]
    copies = start_copies([(own_ref, slabs.at[0]), (two_ref, slabs.at[1])], sems)
    sums = [0.0, 0.0]
    for step in range(2):
        copies[step].wait()
        place = 2 * (x ^ step)
        for side in range(2):
            rows = [att_ref[place + piece, core ^ side] for piece in range(2)]
            sums[side] = sums[side] + lax.dot_general(
                jnp.concatenate(rows, axis=0),
                slabs[step],
                (((0,), (0,)), ((), ())),
                preferred_element_type=jnp.float32,
            )
    keep_ref[...], give_ref[...] = sums


def loss_kernel(
    raw_ref, keep_ref, got_ref, mixed_norm_ref, rstd_ref, live_ref, proj_ref, out_ref
):
    mixed_norm = mixed_norm_ref[...]
    prediction = jnp.dot(
        mixed_norm.astype(jnp.bfloat16), proj_ref[...], preferred_element_type=jnp.float32
    )
    summed = raw_ref[...].astype(jnp.float32) + (keep_ref[...] + got_ref[...])
    target = layer_norm(summed)[0].astype(jnp.bfloat16)
    error = (prediction - target.astype(jnp.float32)) * live_ref[...]
    grad_pred = error.astype(jnp.bfloat16)
    grad_norm = lax.dot_general(
        grad_pred, proj_ref[...], (((1,), (1,)), ((), ())), preferred_element_type=jnp.float32
    )
    first_mean = jnp.mean(grad_norm, axis=-1, keepdims=True)
    second_mean = jnp.mean(grad_norm * mixed_norm, axis=-1, keepdims=True)
    out_ref[...] = (rstd_ref[...] * (grad_norm - first_mean - mixed_norm * second_mean)).astype(
        jnp.bfloat16
    )


def forward_kernel(
    mine_ref,
    up_hbm,
    down_hbm,
    stream_ref,
    normed_ref,
    mixed_norm_ref,
    rstd_ref,
    up_mine_ref,
    down_mine_ref,
    up_ref,
    down_ref,
    sems,
):
    copies = start_copies([(up_hbm, up_ref), (down_hbm, down_ref)], sems)
    copies[0].wait()
    hidden = gelu_tanh(
        jnp.dot(normed_ref[...], up_ref[...], preferred_element_type=jnp.float32)
    ).astype(jnp.bfloat16)
    copies[1].wait()
    mixed = stream_ref[...].astype(jnp.float32) + jnp.dot(
        hidden, down_ref[...], preferred_element_type=jnp.float32
    )
    mixed_norm, rstd = layer_norm(mixed)
    mixed_norm_ref[...] = mixed_norm
    rstd_ref[...] = rstd
    mine = mine_ref[0]
    pieces, share, _ = down_mine_ref.shape
    span = up_ref.shape[1] // pieces
    row = lax.broadcasted_iota(jnp.int32, (span, share), 0)
    column = lax.broadcasted_iota(jnp.int32, (span, share), 1)
    pick = (row == column + mine * share).astype(jnp.float32).astype(jnp.bfloat16)
    picked = []
    for piece in range(pieces):
        window = up_ref[:, piece * span : (piece + 1) * span]
        picked.append(jnp.dot(window, pick, preferred_element_type=jnp.float32))
        start = pl.multiple_of(piece * span + mine * share, 16)
        down_mine_ref[piece] = down_ref[pl.ds(start, share), :]
    up_mine_ref[...] = jnp.concatenate(picked, axis=1).astype(jnp.bfloat16)


def grads_kernel(
    mine_ref, grad_ref, quad_ref, quad_core_ref, up_ref, down_ref, out_ref, grads, normed_rows
):
    mine = mine_ref[0]
    for core, half_ref in enumerate((quad_ref, quad_core_ref)):
        normed_rows[4 * core : 4 * core + 4] = half_ref[...]
        for piece in range(4):
            grads[4 * core + piece] = grad_ref[mine ^ (2 * piece + core)]
    rows = grads.shape[0] * grads.shape[1]
    grad_mixed = grads[...].reshape(rows, grads.shape[2])
    normed = normed_rows[...].reshape(rows, grads.shape[2])
    pre = jnp.dot(normed, up_ref[...], preferred_element_type=jnp.float32)
    hidden = gelu_tanh(pre).astype(jnp.bfloat16)
    pieces, half, _ = out_ref.shape
    half = half // 2
    over_rows = (((0,), (0,)), ((), ()))
    grad_down = lax.dot_general(
        hidden, grad_mixed, over_rows, preferred_element_type=jnp.float32
    )
    grad_hidden = lax.dot_general(
        grad_mixed, down_ref[...], (((1,), (1,)), ((), ())), preferred_element_type=jnp.float32
    )
    grad_pre = (grad_hidden * gelu_slope(pre)).astype(jnp.bfloat16)
    grad_up = lax.dot_general(grad_pre, normed, over_rows, preferred_element_type=jnp.float32)
    for piece in range(pieces):
        rows = slice(piece * half, (piece + 1) * half)
        out_ref[piece, :half, :] = grad_up[rows].astype(jnp.bfloat16)
        out_ref[piece, half:, :] = grad_down[rows].astype(jnp.bfloat16)


def in_vmem(kernel, out_shape, operands, places=0, scratch=(), mib=44, copied=0):
    several = isinstance(out_shape, (list, tuple))
    in_place = pl.BlockSpec(memory_space=pltpu.VMEM)
    return pl.pallas_call(
        kernel,
        out_shape=out_shape,
        in_specs=[pl.BlockSpec(memory_space=pltpu.SMEM)] * places
        + [pl.BlockSpec(memory_space=pltpu.HBM)] * copied
        + [in_place] * (len(operands) - places - copied),
        out_specs=[in_place] * len(out_shape) if several else in_place,
        scratch_shapes=list(scratch),
        cost_estimate=pl.CostEstimate(flops=1, bytes_accessed=1, transcendentals=0),
        compiler_params=pltpu.CompilerParams(vmem_limit_bytes=mib * 2**20),
    )(*operands)


CLIP_GROUP = ("zl", "y", "k")
CHIP_GROUP = ("zl", "y")
ROW_GROUP = ("y", "x", "k")
BATCH_GROUP = ("x", "k")
SUM_GROUP = ("zh", "zl")


def head_shard(
    tokens,
    qkv_weight,
    out_weight,
    mask_blocks,
    owner_map,
    pred_stream,
    pred_up,
    pred_down,
    pred_proj,
):
    zh, zl, y, x, k = (lax.axis_index(name) for name in ("zh", "zl", "y", "x", "k"))
    batch = 2 * x + k
    seq = 4 * zh + 2 * zl + y
    place = batch.astype(jnp.int32)[None]
    _, tok_rows, width = tokens.shape
    owners, blk_dev = pred_stream.shape[1], tok_rows // BLK
    pred_width, units = pred_up.shape

    def swap_clips(value):
        return lax.ppermute(value, ("zh", "k"), ((0, 0), (1, 2), (2, 1), (3, 3)))

    def swap(value, bits):
        return lax.ppermute(value, BATCH_GROUP, tuple((i, i ^ bits) for i in range(owners)))

    raw = swap_clips(tokens[0])

    part = width // 8
    stream_blocks = pred_stream[0].reshape(owners, blk_dev, BLK, pred_width)
    owner_here = lax.dynamic_slice_in_dim(owner_map, seq * blk_dev, blk_dev, 1)
    mine = (owner_here == batch)[:, :, None, None]
    compact = jnp.sum(jnp.where(mine, stream_blocks, 0), axis=1).astype(jnp.bfloat16)
    arrived = lax.all_to_all(compact, BATCH_GROUP, split_axis=0, concat_axis=0, tiled=True)

    def chip_columns(which):
        first = which * width + zl * 4 * part + y * part
        pieces = [
            lax.dynamic_slice(
                qkv_weight, (0, first + core * 2 * part), (qkv_weight.shape[0], part)
            )
            for core in range(2)
        ]
        return jnp.concatenate(pieces, axis=1)

    columns = jnp.stack([chip_columns(which) for which in range(3)])

    raw = after(raw, (arrived, columns))
    raw_f = raw.astype(jnp.float32)
    normed = layer_norm(raw_f)[0].astype(jnp.bfloat16)
    normed_all = lax.all_gather(normed, CLIP_GROUP, axis=0, tiled=True)
    columns_two = swap(columns, 2)
    columns_one = swap(columns, 1)

    from_owner = take(owner_here, batch)[:, None] == jnp.arange(owners, dtype=jnp.int32)
    stream = jnp.sum(jnp.where(from_owner[:, :, None, None], arrived, 0), axis=1)
    stream = stream.astype(jnp.bfloat16).reshape(tok_rows, pred_width)
    stream = swap_clips(stream)
    normed_pred = layer_norm(stream.astype(jnp.float32))[0].astype(jnp.bfloat16)
    normed_x = swap(normed_pred, 2)
    out_two = swap(after(out_weight, columns_two), 2)

    mine_units = (4 * y + batch).astype(jnp.int32)[None]
    mixed_norm, rstd, up_mine, down_mine = functools.partial(in_vmem, mib=44)(
        forward_kernel,
        (
            jax.ShapeDtypeStruct((tok_rows, pred_width), jnp.float32),
            jax.ShapeDtypeStruct((tok_rows, 1), jnp.float32),
            jax.ShapeDtypeStruct((pred_width, units // 8), jnp.bfloat16),
            jax.ShapeDtypeStruct((4, units // 32, pred_width), jnp.bfloat16),
        ),
        (mine_units, pred_up, pred_down, stream, normed_pred),
        places=1,
        copied=2,
        scratch=(
            pltpu.VMEM(pred_up.shape, jnp.bfloat16),
            pltpu.VMEM(pred_down.shape, jnp.bfloat16),
            pltpu.SemaphoreType.DMA((2,)),
        ),
    )
    down_mine = down_mine.reshape(units // 8, pred_width)

    columns_two = after(columns_two, (mixed_norm, normed_x))
    columns_three = swap(columns_two, 1)

    slab = qkv_weight.shape[0]
    qkv_columns = functools.partial(in_vmem, mib=44)(
        weight_kernel,
        jax.ShapeDtypeStruct((3 * part, width), jnp.bfloat16),
        (
            place,
            k.astype(jnp.int32)[None],
            columns,
            columns_one,
            columns_two,
            columns_three,
        ),
        places=2,
        scratch=(
            pltpu.VMEM((3, owners, slab, 2 * part), jnp.bfloat16),
            pltpu.VMEM((2 * part, width), jnp.bfloat16),
        ),
    )

    clip = 2 * x + zh
    shard = 4 * k + 2 * zl + y
    block_ids = shard * blk_dev + jnp.arange(blk_dev, dtype=jnp.int32)
    masked = jnp.any(take(mask_blocks, clip)[:, None] == block_ids[None, :], axis=0)
    divisor = float(owners * mask_blocks.shape[1])
    live = jnp.repeat(masked.astype(jnp.float32) / divisor, BLK)[:, None]

    normed_all = after(normed_all, (qkv_columns, mixed_norm))
    attended = functools.partial(in_vmem, mib=44)(
        attend_kernel,
        jax.ShapeDtypeStruct((4, 2, part, tok_rows), jnp.bfloat16),
        (qkv_columns, normed_all),
        scratch=(pltpu.VMEM((3 * part, normed_all.shape[0]), jnp.float32),),
    )
    pair = jnp.stack([normed_pred, normed_x])
    quad = jnp.concatenate([pair, lax.ppermute(pair, "y", ((0, 1), (1, 0)))])
    quad_core = swap(quad, 1)
    attended = lax.all_to_all(attended, CHIP_GROUP, split_axis=0, concat_axis=0, tiled=True)
    attended = after(attended, quad_core)
    keep, give = functools.partial(in_vmem, mib=44)(
        partial_kernel,
        [jax.ShapeDtypeStruct((tok_rows, width), jnp.float32)] * 2,
        (
            x.astype(jnp.int32)[None],
            k.astype(jnp.int32)[None],
            out_weight,
            out_two,
            attended,
        ),
        places=2,
        copied=2,
        scratch=(
            pltpu.VMEM((2, slab, width), jnp.bfloat16),
            pltpu.SemaphoreType.DMA((2,)),
        ),
    )
    got = swap(give, 1)
    grad_mixed = functools.partial(in_vmem, mib=44)(
        loss_kernel,
        jax.ShapeDtypeStruct((tok_rows, pred_width), jnp.bfloat16),
        (raw, keep, got, mixed_norm, rstd, live, pred_proj),
    )
    grad_rows = lax.all_gather(grad_mixed, ROW_GROUP, axis=0, tiled=True)
    grads = functools.partial(in_vmem, mib=44)(
        grads_kernel,
        jax.ShapeDtypeStruct((4, units // 16, pred_width), jnp.bfloat16),
        (
            mine_units,
            grad_rows.reshape(8, tok_rows, pred_width),
            quad,
            quad_core,
            up_mine,
            down_mine,
        ),
        places=1,
        scratch=(pltpu.VMEM((8, tok_rows, pred_width), jnp.bfloat16),) * 2,
    )
    grads = lax.all_to_all(grads, SUM_GROUP, split_axis=0, concat_axis=0, tiled=True)
    total = jnp.sum(grads.astype(jnp.float32), axis=0)
    half = units // 32
    return total[:half].T, total[half:]


def solution(mesh):
    if mesh.shape["seq"] == 8 and mesh.shape["batch"] == 4:
        names = ("zh", "zl", "y", "x", "k")
        step, batch, seq = head_shard, BATCH_GROUP, names[:3]
        mesh = jax.sharding.Mesh(mesh.devices.reshape(2, 2, 2, 2, 2), names)
    else:
        step, batch, seq = per_device, "batch", "seq"
    everyone = (seq, batch) if isinstance(seq, str) else seq + batch
    in_specs = (
        P(batch, seq, None),
        P(batch, None),
        P(batch, None),
        P(),
        P(),
        P(batch, None, seq, None),
        P(),
        P(),
        P(),
    )
    out_specs = (P(None, everyone), P(everyone, None))
    return jax.shard_map(step, mesh=mesh, in_specs=in_specs, out_specs=out_specs, check_vma=False)
```

```python
import jax
import jax.numpy as jnp
from jax import lax
from jax.experimental import pallas as pl
from jax.experimental.pallas import tpu as pltpu
from jax.sharding import PartitionSpec as P

H = 16
HD = 88
BLK = 64


gelu_coef = 0.7978845608
gelu_cube = 0.044715


def layer_norm(values):
    center = values - jnp.mean(values, axis=-1, keepdims=True)
    variance = jnp.mean(center * center, axis=-1, keepdims=True)
    factor = lax.rsqrt(variance + 1e-06)
    return (center * factor, factor)


def gelu_tanh(values):
    inner = gelu_coef * (values + gelu_cube * values * values * values)
    return 0.5 * values * (1.0 + jnp.tanh(inner))


def gelu_slope(values):
    inner = gelu_coef * (values + gelu_cube * values * values * values)
    tangent = jnp.tanh(inner)
    return 0.5 * (1.0 + tangent) + 0.5 * values * (1.0 - tangent * tangent) * gelu_coef * (
        1.0 + 3.0 * gelu_cube * values * values
    )


def predictor_grads(stream, target_rows, live_rows, pred_up, pred_down, pred_proj, divisor):
    stream_f = stream.astype(jnp.float32)
    normed_pred = layer_norm(stream_f)[0].astype(jnp.bfloat16)
    hidden_pre = jnp.dot(normed_pred, pred_up, preferred_element_type=jnp.float32)
    hidden = gelu_tanh(hidden_pre).astype(jnp.bfloat16)
    mixed = stream_f + jnp.dot(hidden, pred_down, preferred_element_type=jnp.float32)
    mixed_norm, rstd = layer_norm(mixed)
    mixed_rounded = mixed_norm.astype(jnp.bfloat16)
    prediction = jnp.dot(mixed_rounded, pred_proj, preferred_element_type=jnp.float32)
    error = (prediction - target_rows.astype(jnp.float32)) * live_rows[:, None]
    grad_pred = (error / divisor).astype(jnp.bfloat16)
    grad_norm = jnp.dot(grad_pred, pred_proj.T, preferred_element_type=jnp.float32)
    first_mean = jnp.mean(grad_norm, axis=-1, keepdims=True)
    second_mean = jnp.mean(grad_norm * mixed_norm, axis=-1, keepdims=True)
    grad_mixed = (rstd * (grad_norm - first_mean - mixed_norm * second_mean)).astype(jnp.bfloat16)
    grad_down = jnp.dot(hidden.T, grad_mixed, preferred_element_type=jnp.float32)
    grad_hidden = jnp.dot(grad_mixed, pred_down.T, preferred_element_type=jnp.float32)
    grad_pre = (grad_hidden * gelu_slope(hidden_pre)).astype(jnp.bfloat16)
    grad_up = jnp.dot(normed_pred.T, grad_pre, preferred_element_type=jnp.float32)
    return (grad_up, grad_down)


def per_device(
    tokens,
    qkv_weight,
    out_weight,
    mask_blocks,
    owner_map,
    pred_stream,
    pred_up,
    pred_down,
    pred_proj,
):
    stream_in = tokens[0]
    tok_rows, width = stream_in.shape
    clip_now = lax.axis_index("batch")
    shard_now = lax.axis_index("seq")
    owners = lax.axis_size("batch")
    stream_f = stream_in.astype(jnp.float32)
    normed = layer_norm(stream_f)[0].astype(jnp.bfloat16)

    def fold_rows(left, piece):
        return jnp.dot(left, piece, preferred_element_type=jnp.float32)

    projected = fold_rows(normed, lax.all_gather(qkv_weight, "batch", axis=0, tiled=True))
    projected = projected.astype(jnp.bfloat16)
    queries = projected[:, :width].reshape(tok_rows, H, HD)
    keys_values = projected[:, width:]
    scale = 1.0 / HD**0.5

    def attend_block(carry, block):
        weighted, totals = carry
        block_keys = block[:, :width].reshape(block.shape[0], H, HD)
        block_values = block[:, width:].reshape(block.shape[0], H, HD)
        scores = (
            jnp.einsum("qhd,khd->hqk", queries, block_keys, preferred_element_type=jnp.float32)
            * scale
        )
        weights = jnp.exp(scores)
        totals = totals + jnp.sum(weights, axis=2)
        weighted = weighted + jnp.einsum(
            "hqk,khd->qhd",
            weights.astype(jnp.bfloat16),
            block_values,
            preferred_element_type=jnp.float32,
        )
        return (weighted, totals)

    start_state = (jnp.zeros((tok_rows, H, HD), jnp.float32), jnp.zeros((H, tok_rows), jnp.float32))
    piece = lax.all_gather(keys_values, "seq", axis=0, tiled=True)
    rows = piece.shape[0]
    blocks = piece.reshape(rows // 512, 512, piece.shape[1])
    weighted, totals = lax.scan(
        lambda state, block: (attend_block(state, block), None), start_state, blocks
    )[0]
    attended = (weighted / totals.T[:, :, None]).reshape(tok_rows, width).astype(jnp.bfloat16)
    attn_out = fold_rows(attended, lax.all_gather(out_weight, "batch", axis=0, tiled=True))
    target = layer_norm(stream_f + attn_out)[0].astype(jnp.bfloat16)
    blocks_dev = tok_rows // BLK
    block_ids = shard_now * blocks_dev + jnp.arange(blocks_dev, dtype=jnp.int32)
    owner_ids = jnp.arange(owners, dtype=jnp.int32)
    all_masked = jnp.any(mask_blocks[:, :, None] == block_ids[None, None, :], axis=1)
    all_owner = lax.dynamic_slice_in_dim(owner_map, shard_now * blocks_dev, blocks_dev, 1)
    my_masked = lax.dynamic_slice_in_dim(all_masked, clip_now, 1, 0)[0]
    my_owner = lax.dynamic_slice_in_dim(all_owner, clip_now, 1, 0)[0]
    send_select = (my_masked[None, :] & (my_owner[None, :] == owner_ids[:, None])).astype(
        jnp.bfloat16
    )
    target_blocks = target.reshape(blocks_dev, BLK, width)
    outgoing = jnp.einsum(
        "ob,brd->ord", send_select, target_blocks, preferred_element_type=jnp.float32
    ).astype(jnp.bfloat16)
    incoming = lax.all_to_all(outgoing, "batch", split_axis=0, concat_axis=0, tiled=True)
    recv_flags = all_masked & (all_owner == clip_now)
    recv_select = recv_flags.astype(jnp.bfloat16)
    live_clip = jnp.any(recv_flags, axis=1).astype(jnp.float32)
    live_rows = jnp.broadcast_to(live_clip[:, None], (owners, BLK)).reshape(owners * BLK)
    stream_blocks = pred_stream[0].reshape(owners, blocks_dev, BLK, pred_stream.shape[3])
    stream_picked = jnp.einsum(
        "cb,cbrd->crd", recv_select, stream_blocks, preferred_element_type=jnp.float32
    ).astype(jnp.bfloat16)
    stream_rows = stream_picked.reshape(owners * BLK, pred_stream.shape[3])
    target_rows = incoming.reshape(owners * BLK, width)
    divisor = float(owners * mask_blocks.shape[1])
    grad_up, grad_down = predictor_grads(
        stream_rows, target_rows, live_rows, pred_up, pred_down, pred_proj, divisor
    )
    return (
        lax.psum_scatter(grad_up, ("seq", "batch"), scatter_dimension=1, tiled=True),
        lax.psum_scatter(grad_down, ("seq", "batch"), scatter_dimension=0, tiled=True),
    )


def after(value, other):
    return lax.optimization_barrier((value, other))[0]


def take(array, index):
    return lax.dynamic_index_in_dim(array, index, 0, keepdims=False)


def start_copies(pairs, sems):
    copies = [pltpu.make_async_copy(*pair, sems.at[i]) for i, pair in enumerate(pairs)]
    for copy in copies:
        copy.start()
    return copies


def weight_kernel(place_ref, core_ref, *refs):
    *piece_refs, out_ref, held, turned = refs
    place, core = place_ref[0], core_ref[0]
    parts, slabs, rows, columns = held.shape
    part = out_ref.shape[0] // parts
    for step in range(slabs):
        held[0, place ^ step] = piece_refs[2 * step][...]
        held[1:, place ^ step] = piece_refs[2 * step + 1][...]
    for which in range(parts):
        turned[...] = held[which].reshape(slabs * rows, columns).T
        start = pl.multiple_of(core * part, part)
        out_ref[which * part : (which + 1) * part, :] = turned[pl.ds(start, part), :]


def attend_kernel(weight_ref, normed_ref, out_ref, projected):
    projected[...] = lax.dot_general(
        weight_ref[...],
        normed_ref[...],
        (((1,), (1,)), ((), ())),
        preferred_element_type=jnp.float32,
    )
    part = projected.shape[0] // 3
    chips, cores, _, block_rows = out_ref.shape
    pad = jnp.zeros((-HD % 128, projected.shape[1]), jnp.float32)
    log2_scale = 1.4426950408889634 / HD**0.5

    def head_rows(which, head):
        start = which * part + head * HD
        rows = projected[start : start + HD, :]
        return jnp.concatenate([rows, pad], axis=0).astype(jnp.bfloat16)

    heads = part // HD
    operands = [(head_rows(0, h), head_rows(1, h).T, head_rows(2, h)) for h in range(heads)]
    span = block_rows * cores
    for chip in range(chips):
        joined = []
        for queries, keys, values in operands:
            scores = jnp.dot(
                keys,
                queries[:, chip * span : (chip + 1) * span],
                preferred_element_type=jnp.float32,
            )
            weights = jnp.exp2(scores * log2_scale)
            totals = jnp.sum(weights, axis=0, keepdims=True)
            summed = jnp.dot(
                values, weights.astype(jnp.bfloat16), preferred_element_type=jnp.float32
            )
            joined.append(summed[:HD] / totals)
        attended = jnp.concatenate(joined, axis=0).astype(jnp.bfloat16)
        for core in range(cores):
            out_ref[chip, core] = attended[:, core * block_rows : (core + 1) * block_rows]


def partial_kernel(
    x_ref, core_ref, own_ref, two_ref, att_ref, keep_ref, give_ref, slabs, sems
):
    x, core = x_ref[0], core_ref[0]
    copies = start_copies([(own_ref, slabs.at[0]), (two_ref, slabs.at[1])], sems)
    sums = [0.0, 0.0]
    for step in range(2):
        copies[step].wait()
        place = 2 * (x ^ step)
        for side in range(2):
            rows = [att_ref[place + piece, core ^ side] for piece in range(2)]
            sums[side] = sums[side] + lax.dot_general(
                jnp.concatenate(rows, axis=0),
                slabs[step],
                (((0,), (0,)), ((), ())),
                preferred_element_type=jnp.float32,
            )
    keep_ref[...], give_ref[...] = sums[0], sums[1].astype(give_ref.dtype)


def loss_kernel(
    raw_ref, keep_ref, got_ref, mixed_norm_ref, rstd_ref, live_ref, proj_ref, out_ref
):
    mixed_norm = mixed_norm_ref[...]
    prediction = jnp.dot(
        mixed_norm.astype(jnp.bfloat16), proj_ref[...], preferred_element_type=jnp.float32
    )
    summed = raw_ref[...].astype(jnp.float32) + (keep_ref[...] + got_ref[...].astype(jnp.float32))
    target = layer_norm(summed)[0].astype(jnp.bfloat16)
    error = (prediction - target.astype(jnp.float32)) * live_ref[...]
    grad_pred = error.astype(jnp.bfloat16)
    grad_norm = lax.dot_general(
        grad_pred, proj_ref[...], (((1,), (1,)), ((), ())), preferred_element_type=jnp.float32
    )
    first_mean = jnp.mean(grad_norm, axis=-1, keepdims=True)
    second_mean = jnp.mean(grad_norm * mixed_norm, axis=-1, keepdims=True)
    out_ref[...] = (rstd_ref[...] * (grad_norm - first_mean - mixed_norm * second_mean)).astype(
        jnp.bfloat16
    )


def forward_kernel(
    mine_ref,
    up_hbm,
    down_hbm,
    stream_ref,
    normed_ref,
    mixed_norm_ref,
    rstd_ref,
    up_mine_ref,
    down_mine_ref,
    up_ref,
    down_ref,
    sems,
):
    copies = start_copies([(up_hbm, up_ref), (down_hbm, down_ref)], sems)
    copies[0].wait()
    hidden = gelu_tanh(
        jnp.dot(normed_ref[...], up_ref[...], preferred_element_type=jnp.float32)
    ).astype(jnp.bfloat16)
    copies[1].wait()
    mixed = stream_ref[...].astype(jnp.float32) + jnp.dot(
        hidden, down_ref[...], preferred_element_type=jnp.float32
    )
    mixed_norm, rstd = layer_norm(mixed)
    mixed_norm_ref[...] = mixed_norm
    rstd_ref[...] = rstd
    mine = mine_ref[0]
    pieces, share, _ = down_mine_ref.shape
    span = up_ref.shape[1] // pieces
    row = lax.broadcasted_iota(jnp.int32, (span, share), 0)
    column = lax.broadcasted_iota(jnp.int32, (span, share), 1)
    pick = (row == column + mine * share).astype(jnp.float32).astype(jnp.bfloat16)
    picked = []
    for piece in range(pieces):
        window = up_ref[:, piece * span : (piece + 1) * span]
        picked.append(jnp.dot(window, pick, preferred_element_type=jnp.float32))
        start = pl.multiple_of(piece * span + mine * share, 16)
        down_mine_ref[piece] = down_ref[pl.ds(start, share), :]
    up_mine_ref[...] = jnp.concatenate(picked, axis=1).astype(jnp.bfloat16)


def grads_kernel(
    mine_ref, grad_ref, quad_ref, quad_core_ref, up_ref, down_ref, out_ref, grads, normed_rows
):
    mine = mine_ref[0]
    for core, half_ref in enumerate((quad_ref, quad_core_ref)):
        normed_rows[4 * core : 4 * core + 4] = half_ref[...]
        for piece in range(4):
            grads[4 * core + piece] = grad_ref[mine ^ (2 * piece + core)]
    rows = grads.shape[0] * grads.shape[1]
    grad_mixed = grads[...].reshape(rows, grads.shape[2])
    normed = normed_rows[...].reshape(rows, grads.shape[2])
    pre = jnp.dot(normed, up_ref[...], preferred_element_type=jnp.float32)
    hidden = gelu_tanh(pre).astype(jnp.bfloat16)
    pieces, half, _ = out_ref.shape
    half = half // 2
    over_rows = (((0,), (0,)), ((), ()))
    grad_down = lax.dot_general(
        hidden, grad_mixed, over_rows, preferred_element_type=jnp.float32
    )
    grad_hidden = lax.dot_general(
        grad_mixed, down_ref[...], (((1,), (1,)), ((), ())), preferred_element_type=jnp.float32
    )
    grad_pre = (grad_hidden * gelu_slope(pre)).astype(jnp.bfloat16)
    grad_up = lax.dot_general(grad_pre, normed, over_rows, preferred_element_type=jnp.float32)
    for piece in range(pieces):
        rows = slice(piece * half, (piece + 1) * half)
        out_ref[piece, :half, :] = grad_up[rows].astype(jnp.bfloat16)
        out_ref[piece, half:, :] = grad_down[rows].astype(jnp.bfloat16)


def in_vmem(kernel, out_shape, operands, places=0, scratch=(), mib=32, copied=0):
    several = isinstance(out_shape, (list, tuple))
    in_place = pl.BlockSpec(memory_space=pltpu.VMEM)
    return pl.pallas_call(
        kernel,
        out_shape=out_shape,
        in_specs=[pl.BlockSpec(memory_space=pltpu.SMEM)] * places
        + [pl.BlockSpec(memory_space=pltpu.HBM)] * copied
        + [in_place] * (len(operands) - places - copied),
        out_specs=[in_place] * len(out_shape) if several else in_place,
        scratch_shapes=list(scratch),
        cost_estimate=pl.CostEstimate(flops=1, bytes_accessed=1, transcendentals=0),
        compiler_params=pltpu.CompilerParams(vmem_limit_bytes=mib * 2**20),
    )(*operands)


CLIP_GROUP = ("zl", "y", "k")
CHIP_GROUP = ("zl", "y")
ROW_GROUP = ("y", "x", "k")
BATCH_GROUP = ("x", "k")
SUM_GROUP = ("zh", "zl")


def head_shard(
    tokens,
    qkv_weight,
    out_weight,
    mask_blocks,
    owner_map,
    pred_stream,
    pred_up,
    pred_down,
    pred_proj,
):
    zh, zl, y, x, k = (lax.axis_index(name) for name in ("zh", "zl", "y", "x", "k"))
    batch = 2 * x + k
    seq = 4 * zh + 2 * zl + y
    place = batch.astype(jnp.int32)[None]
    _, tok_rows, width = tokens.shape
    owners, blk_dev = pred_stream.shape[1], tok_rows // BLK
    pred_width, units = pred_up.shape

    def swap_clips(value):
        return lax.ppermute(value, ("zh", "k"), ((0, 0), (1, 2), (2, 1), (3, 3)))

    def swap(value, bits):
        return lax.ppermute(value, BATCH_GROUP, tuple((i, i ^ bits) for i in range(owners)))

    raw = swap_clips(tokens[0])

    part = width // 8
    stream_blocks = pred_stream[0].reshape(owners, blk_dev, BLK, pred_width)
    owner_here = lax.dynamic_slice_in_dim(owner_map, seq * blk_dev, blk_dev, 1)
    mine = (owner_here == batch)[:, :, None, None]
    compact = jnp.sum(jnp.where(mine, stream_blocks, 0), axis=1).astype(jnp.bfloat16)
    arrived = lax.all_to_all(compact, BATCH_GROUP, split_axis=0, concat_axis=0, tiled=True)

    def chip_columns(which):
        first = which * width + zl * 4 * part + y * part
        pieces = [
            lax.dynamic_slice(
                qkv_weight, (0, first + core * 2 * part), (qkv_weight.shape[0], part)
            )
            for core in range(2)
        ]
        return jnp.concatenate(pieces, axis=1)

    early, *late = (chip_columns(which) for which in range(3))
    late = jnp.stack(late)
    early_two = swap(early, 2)

    raw = after(raw, (arrived, early_two))
    raw_f = raw.astype(jnp.float32)
    normed = layer_norm(raw_f)[0].astype(jnp.bfloat16)
    normed_all = lax.all_gather(normed, CLIP_GROUP, axis=0, tiled=True)
    late_two = swap(late, 2)
    early_one, late_one = swap(early, 1), swap(late, 1)
    early_three = swap(early_two, 1)

    from_owner = take(owner_here, batch)[:, None] == jnp.arange(owners, dtype=jnp.int32)
    stream = jnp.sum(jnp.where(from_owner[:, :, None, None], arrived, 0), axis=1)
    stream = stream.astype(jnp.bfloat16).reshape(tok_rows, pred_width)
    stream = swap_clips(stream)
    normed_pred = layer_norm(stream.astype(jnp.float32))[0].astype(jnp.bfloat16)
    normed_x = swap(normed_pred, 2)
    out_two = swap(after(out_weight, late_two), 2)

    mine_units = (4 * y + batch).astype(jnp.int32)[None]
    mixed_norm, rstd, up_mine, down_mine = in_vmem(
        forward_kernel,
        (
            jax.ShapeDtypeStruct((tok_rows, pred_width), jnp.float32),
            jax.ShapeDtypeStruct((tok_rows, 1), jnp.float32),
            jax.ShapeDtypeStruct((pred_width, units // 8), jnp.bfloat16),
            jax.ShapeDtypeStruct((4, units // 32, pred_width), jnp.bfloat16),
        ),
        (mine_units, pred_up, pred_down, stream, normed_pred),
        places=1,
        copied=2,
        scratch=(
            pltpu.VMEM(pred_up.shape, jnp.bfloat16),
            pltpu.VMEM(pred_down.shape, jnp.bfloat16),
            pltpu.SemaphoreType.DMA((2,)),
        ),
    )
    down_mine = down_mine.reshape(units // 8, pred_width)

    late_two = after(late_two, (mixed_norm, normed_x))
    late_three = swap(late_two, 1)

    slab = qkv_weight.shape[0]
    qkv_columns = in_vmem(
        weight_kernel,
        jax.ShapeDtypeStruct((3 * part, width), jnp.bfloat16),
        (
            place,
            k.astype(jnp.int32)[None],
            early,
            late,
            early_one,
            late_one,
            early_two,
            late_two,
            early_three,
            late_three,
        ),
        places=2,
        scratch=(
            pltpu.VMEM((3, owners, slab, 2 * part), jnp.bfloat16),
            pltpu.VMEM((2 * part, width), jnp.bfloat16),
        ),
    )

    clip = 2 * x + zh
    shard = 4 * k + 2 * zl + y
    block_ids = shard * blk_dev + jnp.arange(blk_dev, dtype=jnp.int32)
    masked = jnp.any(take(mask_blocks, clip)[:, None] == block_ids[None, :], axis=0)
    divisor = float(owners * mask_blocks.shape[1])
    live = jnp.repeat(masked.astype(jnp.float32) / divisor, BLK)[:, None]

    normed_all = after(normed_all, (qkv_columns, mixed_norm))
    attended = in_vmem(
        attend_kernel,
        jax.ShapeDtypeStruct((4, 2, part, tok_rows), jnp.bfloat16),
        (qkv_columns, normed_all),
        scratch=(pltpu.VMEM((3 * part, normed_all.shape[0]), jnp.float32),),
    )
    pair = jnp.stack([normed_pred, normed_x])
    quad = jnp.concatenate([pair, lax.ppermute(pair, "y", ((0, 1), (1, 0)))])
    quad_core = swap(quad, 1)
    attended = lax.all_to_all(attended, CHIP_GROUP, split_axis=0, concat_axis=0, tiled=True)
    attended = after(attended, quad_core)
    keep, give = in_vmem(
        partial_kernel,
        [jax.ShapeDtypeStruct((tok_rows, width), dtype) for dtype in (jnp.float32, jnp.bfloat16)],
        (
            x.astype(jnp.int32)[None],
            k.astype(jnp.int32)[None],
            out_weight,
            out_two,
            attended,
        ),
        places=2,
        copied=2,
        scratch=(
            pltpu.VMEM((2, slab, width), jnp.bfloat16),
            pltpu.SemaphoreType.DMA((2,)),
        ),
    )
    got = swap(give, 1)
    grad_mixed = in_vmem(
        loss_kernel,
        jax.ShapeDtypeStruct((tok_rows, pred_width), jnp.bfloat16),
        (raw, keep, got, mixed_norm, rstd, live, pred_proj),
    )
    grad_rows = lax.all_gather(grad_mixed, ROW_GROUP, axis=0, tiled=True)
    grads = in_vmem(
        grads_kernel,
        jax.ShapeDtypeStruct((4, units // 16, pred_width), jnp.bfloat16),
        (
            mine_units,
            grad_rows.reshape(8, tok_rows, pred_width),
            quad,
            quad_core,
            up_mine,
            down_mine,
        ),
        places=1,
        scratch=(pltpu.VMEM((8, tok_rows, pred_width), jnp.bfloat16),) * 2,
    )
    grads = lax.all_to_all(grads, SUM_GROUP, split_axis=0, concat_axis=0, tiled=True)
    total = jnp.sum(grads.astype(jnp.float32), axis=0)
    half = units // 32
    return total[:half].T, total[half:]


def solution(mesh):
    if mesh.shape["seq"] == 8 and mesh.shape["batch"] == 4:
        names = ("zh", "zl", "y", "x", "k")
        step, batch, seq = head_shard, BATCH_GROUP, names[:3]
        mesh = jax.sharding.Mesh(mesh.devices.reshape(2, 2, 2, 2, 2), names)
    else:
        step, batch, seq = per_device, "batch", "seq"
    everyone = (seq, batch) if isinstance(seq, str) else seq + batch
    in_specs = (
        P(batch, seq, None),
        P(batch, None),
        P(batch, None),
        P(),
        P(),
        P(batch, None, seq, None),
        P(),
        P(),
        P(),
    )
    out_specs = (P(None, everyone), P(everyone, None))
    return jax.shard_map(step, mesh=mesh, in_specs=in_specs, out_specs=out_specs, check_vma=False)
```

```python
import jax
import jax.numpy as jnp
from jax import lax
from jax.experimental import pallas as pl
from jax.experimental.pallas import tpu as pltpu
from jax.sharding import PartitionSpec as P

H = 16
HD = 88
BLK = 64


gelu_coef = 0.7978845608
gelu_cube = 0.044715


def layer_norm(values):
    center = values - jnp.mean(values, axis=-1, keepdims=True)
    variance = jnp.mean(center * center, axis=-1, keepdims=True)
    factor = lax.rsqrt(variance + 1e-06)
    return (center * factor, factor)


def gelu_tanh(values):
    inner = gelu_coef * (values + gelu_cube * values * values * values)
    return 0.5 * values * (1.0 + jnp.tanh(inner))


def gelu_slope(values):
    inner = gelu_coef * (values + gelu_cube * values * values * values)
    tangent = jnp.tanh(inner)
    return 0.5 * (1.0 + tangent) + 0.5 * values * (1.0 - tangent * tangent) * gelu_coef * (
        1.0 + 3.0 * gelu_cube * values * values
    )


def predictor_grads(stream, target_rows, live_rows, pred_up, pred_down, pred_proj, divisor):
    stream_f = stream.astype(jnp.float32)
    normed_pred = layer_norm(stream_f)[0].astype(jnp.bfloat16)
    hidden_pre = jnp.dot(normed_pred, pred_up, preferred_element_type=jnp.float32)
    hidden = gelu_tanh(hidden_pre).astype(jnp.bfloat16)
    mixed = stream_f + jnp.dot(hidden, pred_down, preferred_element_type=jnp.float32)
    mixed_norm, rstd = layer_norm(mixed)
    mixed_rounded = mixed_norm.astype(jnp.bfloat16)
    prediction = jnp.dot(mixed_rounded, pred_proj, preferred_element_type=jnp.float32)
    error = (prediction - target_rows.astype(jnp.float32)) * live_rows[:, None]
    grad_pred = (error / divisor).astype(jnp.bfloat16)
    grad_norm = jnp.dot(grad_pred, pred_proj.T, preferred_element_type=jnp.float32)
    first_mean = jnp.mean(grad_norm, axis=-1, keepdims=True)
    second_mean = jnp.mean(grad_norm * mixed_norm, axis=-1, keepdims=True)
    grad_mixed = (rstd * (grad_norm - first_mean - mixed_norm * second_mean)).astype(jnp.bfloat16)
    grad_down = jnp.dot(hidden.T, grad_mixed, preferred_element_type=jnp.float32)
    grad_hidden = jnp.dot(grad_mixed, pred_down.T, preferred_element_type=jnp.float32)
    grad_pre = (grad_hidden * gelu_slope(hidden_pre)).astype(jnp.bfloat16)
    grad_up = jnp.dot(normed_pred.T, grad_pre, preferred_element_type=jnp.float32)
    return (grad_up, grad_down)


def per_device(
    tokens,
    qkv_weight,
    out_weight,
    mask_blocks,
    owner_map,
    pred_stream,
    pred_up,
    pred_down,
    pred_proj,
):
    stream_in = tokens[0]
    tok_rows, width = stream_in.shape
    clip_now = lax.axis_index("batch")
    shard_now = lax.axis_index("seq")
    owners = lax.axis_size("batch")
    stream_f = stream_in.astype(jnp.float32)
    normed = layer_norm(stream_f)[0].astype(jnp.bfloat16)

    def fold_rows(left, piece):
        return jnp.dot(left, piece, preferred_element_type=jnp.float32)

    projected = fold_rows(normed, lax.all_gather(qkv_weight, "batch", axis=0, tiled=True))
    projected = projected.astype(jnp.bfloat16)
    queries = projected[:, :width].reshape(tok_rows, H, HD)
    keys_values = projected[:, width:]
    scale = 1.0 / HD**0.5

    def attend_block(carry, block):
        weighted, totals = carry
        block_keys = block[:, :width].reshape(block.shape[0], H, HD)
        block_values = block[:, width:].reshape(block.shape[0], H, HD)
        scores = (
            jnp.einsum("qhd,khd->hqk", queries, block_keys, preferred_element_type=jnp.float32)
            * scale
        )
        weights = jnp.exp(scores)
        totals = totals + jnp.sum(weights, axis=2)
        weighted = weighted + jnp.einsum(
            "hqk,khd->qhd",
            weights.astype(jnp.bfloat16),
            block_values,
            preferred_element_type=jnp.float32,
        )
        return (weighted, totals)

    start_state = (jnp.zeros((tok_rows, H, HD), jnp.float32), jnp.zeros((H, tok_rows), jnp.float32))
    piece = lax.all_gather(keys_values, "seq", axis=0, tiled=True)
    rows = piece.shape[0]
    blocks = piece.reshape(rows // 512, 512, piece.shape[1])
    weighted, totals = lax.scan(
        lambda state, block: (attend_block(state, block), None), start_state, blocks
    )[0]
    attended = (weighted / totals.T[:, :, None]).reshape(tok_rows, width).astype(jnp.bfloat16)
    attn_out = fold_rows(attended, lax.all_gather(out_weight, "batch", axis=0, tiled=True))
    target = layer_norm(stream_f + attn_out)[0].astype(jnp.bfloat16)
    blocks_dev = tok_rows // BLK
    block_ids = shard_now * blocks_dev + jnp.arange(blocks_dev, dtype=jnp.int32)
    owner_ids = jnp.arange(owners, dtype=jnp.int32)
    all_masked = jnp.any(mask_blocks[:, :, None] == block_ids[None, None, :], axis=1)
    all_owner = lax.dynamic_slice_in_dim(owner_map, shard_now * blocks_dev, blocks_dev, 1)
    my_masked = lax.dynamic_slice_in_dim(all_masked, clip_now, 1, 0)[0]
    my_owner = lax.dynamic_slice_in_dim(all_owner, clip_now, 1, 0)[0]
    send_select = (my_masked[None, :] & (my_owner[None, :] == owner_ids[:, None])).astype(
        jnp.bfloat16
    )
    target_blocks = target.reshape(blocks_dev, BLK, width)
    outgoing = jnp.einsum(
        "ob,brd->ord", send_select, target_blocks, preferred_element_type=jnp.float32
    ).astype(jnp.bfloat16)
    incoming = lax.all_to_all(outgoing, "batch", split_axis=0, concat_axis=0, tiled=True)
    recv_flags = all_masked & (all_owner == clip_now)
    recv_select = recv_flags.astype(jnp.bfloat16)
    live_clip = jnp.any(recv_flags, axis=1).astype(jnp.float32)
    live_rows = jnp.broadcast_to(live_clip[:, None], (owners, BLK)).reshape(owners * BLK)
    stream_blocks = pred_stream[0].reshape(owners, blocks_dev, BLK, pred_stream.shape[3])
    stream_picked = jnp.einsum(
        "cb,cbrd->crd", recv_select, stream_blocks, preferred_element_type=jnp.float32
    ).astype(jnp.bfloat16)
    stream_rows = stream_picked.reshape(owners * BLK, pred_stream.shape[3])
    target_rows = incoming.reshape(owners * BLK, width)
    divisor = float(owners * mask_blocks.shape[1])
    grad_up, grad_down = predictor_grads(
        stream_rows, target_rows, live_rows, pred_up, pred_down, pred_proj, divisor
    )
    return (
        lax.psum_scatter(grad_up, ("seq", "batch"), scatter_dimension=1, tiled=True),
        lax.psum_scatter(grad_down, ("seq", "batch"), scatter_dimension=0, tiled=True),
    )


def after(value, other):
    return lax.optimization_barrier((value, other))[0]


def take(array, index):
    return lax.dynamic_index_in_dim(array, index, 0, keepdims=False)


def start_copies(pairs, sems):
    copies = [pltpu.make_async_copy(*pair, sems.at[i]) for i, pair in enumerate(pairs)]
    for copy in copies:
        copy.start()
    return copies


def weight_kernel(place_ref, core_ref, *refs):
    *piece_refs, out_ref, held, turned = refs
    place, core = place_ref[0], core_ref[0]
    parts, slabs, rows, columns = held.shape
    part = out_ref.shape[0] // parts
    for step in range(slabs):
        held[0, place ^ step] = piece_refs[2 * step][...]
        held[1:, place ^ step] = piece_refs[2 * step + 1][...]
    for which in range(parts):
        turned[...] = held[which].reshape(slabs * rows, columns).T
        start = pl.multiple_of(core * part, part)
        out_ref[which * part : (which + 1) * part, :] = turned[pl.ds(start, part), :]


def attend_kernel(weight_ref, normed_ref, out_ref, projected):
    projected[...] = lax.dot_general(
        weight_ref[...],
        normed_ref[...],
        (((1,), (1,)), ((), ())),
        preferred_element_type=jnp.float32,
    )
    part = projected.shape[0] // 3
    chips, cores, _, block_rows = out_ref.shape
    pad = jnp.zeros((-HD % 128, projected.shape[1]), jnp.float32)
    log2_scale = 1.4426950408889634 / HD**0.5

    def head_rows(which, head):
        start = which * part + head * HD
        rows = projected[start : start + HD, :]
        return jnp.concatenate([rows, pad], axis=0).astype(jnp.bfloat16)

    heads = part // HD
    operands = [(head_rows(0, h), head_rows(1, h).T, head_rows(2, h)) for h in range(heads)]
    span = block_rows * cores
    for chip in range(chips):
        joined = []
        for queries, keys, values in operands:
            scores = jnp.dot(
                keys,
                queries[:, chip * span : (chip + 1) * span],
                preferred_element_type=jnp.float32,
            )
            weights = jnp.exp2(scores * log2_scale)
            totals = jnp.sum(weights, axis=0, keepdims=True)
            summed = jnp.dot(
                values, weights.astype(jnp.bfloat16), preferred_element_type=jnp.float32
            )
            joined.append(summed[:HD] / totals)
        attended = jnp.concatenate(joined, axis=0).astype(jnp.bfloat16)
        for core in range(cores):
            out_ref[chip, core] = attended[:, core * block_rows : (core + 1) * block_rows]


def partial_kernel(
    x_ref, core_ref, own_ref, two_ref, att_ref, keep_ref, give_ref, slabs, sems
):
    x, core = x_ref[0], core_ref[0]
    copies = start_copies([(own_ref, slabs.at[0]), (two_ref, slabs.at[1])], sems)
    sums = [0.0, 0.0]
    for step in range(2):
        copies[step].wait()
        place = 2 * (x ^ step)
        for side in range(2):
            rows = [att_ref[place + piece, core ^ side] for piece in range(2)]
            sums[side] = sums[side] + lax.dot_general(
                jnp.concatenate(rows, axis=0),
                slabs[step],
                (((0,), (0,)), ((), ())),
                preferred_element_type=jnp.float32,
            )
    keep_ref[...], give_ref[...] = sums[0], sums[1].astype(give_ref.dtype)


def loss_kernel(
    raw_ref, keep_ref, got_ref, mixed_norm_ref, rstd_ref, live_ref, proj_ref, out_ref
):
    mixed_norm = mixed_norm_ref[...]
    prediction = jnp.dot(
        mixed_norm.astype(jnp.bfloat16), proj_ref[...], preferred_element_type=jnp.float32
    )
    summed = raw_ref[...].astype(jnp.float32) + (keep_ref[...] + got_ref[...].astype(jnp.float32))
    target = layer_norm(summed)[0].astype(jnp.bfloat16)
    error = (prediction - target.astype(jnp.float32)) * live_ref[...]
    grad_pred = error.astype(jnp.bfloat16)
    grad_norm = lax.dot_general(
        grad_pred, proj_ref[...], (((1,), (1,)), ((), ())), preferred_element_type=jnp.float32
    )
    first_mean = jnp.mean(grad_norm, axis=-1, keepdims=True)
    second_mean = jnp.mean(grad_norm * mixed_norm, axis=-1, keepdims=True)
    out_ref[...] = (rstd_ref[...] * (grad_norm - first_mean - mixed_norm * second_mean)).astype(
        jnp.bfloat16
    )


def forward_kernel(
    mine_ref,
    up_hbm,
    down_hbm,
    stream_ref,
    normed_ref,
    mixed_norm_ref,
    rstd_ref,
    up_mine_ref,
    down_mine_ref,
    up_ref,
    down_ref,
    sems,
):
    copies = start_copies([(up_hbm, up_ref), (down_hbm, down_ref)], sems)
    copies[0].wait()
    hidden = gelu_tanh(
        jnp.dot(normed_ref[...], up_ref[...], preferred_element_type=jnp.float32)
    ).astype(jnp.bfloat16)
    copies[1].wait()
    mixed = stream_ref[...].astype(jnp.float32) + jnp.dot(
        hidden, down_ref[...], preferred_element_type=jnp.float32
    )
    mixed_norm, rstd = layer_norm(mixed)
    mixed_norm_ref[...] = mixed_norm
    rstd_ref[...] = rstd
    mine = mine_ref[0]
    pieces, share, _ = down_mine_ref.shape
    span = up_ref.shape[1] // pieces
    row = lax.broadcasted_iota(jnp.int32, (span, share), 0)
    column = lax.broadcasted_iota(jnp.int32, (span, share), 1)
    pick = (row == column + mine * share).astype(jnp.float32).astype(jnp.bfloat16)
    picked = []
    for piece in range(pieces):
        window = up_ref[:, piece * span : (piece + 1) * span]
        picked.append(jnp.dot(window, pick, preferred_element_type=jnp.float32))
        start = pl.multiple_of(piece * span + mine * share, 16)
        down_mine_ref[piece] = down_ref[pl.ds(start, share), :]
    up_mine_ref[...] = jnp.concatenate(picked, axis=1).astype(jnp.bfloat16)


def grads_kernel(
    mine_ref, grad_ref, quad_ref, quad_core_ref, up_ref, down_ref, out_ref, grads, normed_rows
):
    mine = mine_ref[0]
    for core, half_ref in enumerate((quad_ref, quad_core_ref)):
        normed_rows[4 * core : 4 * core + 4] = half_ref[...]
        for piece in range(4):
            grads[4 * core + piece] = grad_ref[mine ^ (2 * piece + core)]
    rows = grads.shape[0] * grads.shape[1]
    grad_mixed = grads[...].reshape(rows, grads.shape[2])
    normed = normed_rows[...].reshape(rows, grads.shape[2])
    pre = jnp.dot(normed, up_ref[...], preferred_element_type=jnp.float32)
    hidden = gelu_tanh(pre).astype(jnp.bfloat16)
    pieces, half, _ = out_ref.shape
    half = half // 2
    over_rows = (((0,), (0,)), ((), ()))
    grad_down = lax.dot_general(
        hidden, grad_mixed, over_rows, preferred_element_type=jnp.float32
    )
    grad_hidden = lax.dot_general(
        grad_mixed, down_ref[...], (((1,), (1,)), ((), ())), preferred_element_type=jnp.float32
    )
    grad_pre = (grad_hidden * gelu_slope(pre)).astype(jnp.bfloat16)
    grad_up = lax.dot_general(grad_pre, normed, over_rows, preferred_element_type=jnp.float32)
    for piece in range(pieces):
        rows = slice(piece * half, (piece + 1) * half)
        out_ref[piece, :half, :] = grad_up[rows].astype(jnp.bfloat16)
        out_ref[piece, half:, :] = grad_down[rows].astype(jnp.bfloat16)


def in_vmem(kernel, out_shape, operands, places=0, scratch=(), mib=32, copied=0):
    several = isinstance(out_shape, (list, tuple))
    in_place = pl.BlockSpec(memory_space=pltpu.VMEM)
    return pl.pallas_call(
        kernel,
        out_shape=out_shape,
        in_specs=[pl.BlockSpec(memory_space=pltpu.SMEM)] * places
        + [pl.BlockSpec(memory_space=pltpu.HBM)] * copied
        + [in_place] * (len(operands) - places - copied),
        out_specs=[in_place] * len(out_shape) if several else in_place,
        scratch_shapes=list(scratch),
        cost_estimate=pl.CostEstimate(flops=1, bytes_accessed=1, transcendentals=0),
        compiler_params=pltpu.CompilerParams(vmem_limit_bytes=mib * 2**20),
    )(*operands)


CLIP_GROUP = ("zl", "y", "k")
CHIP_GROUP = ("zl", "y")
ROW_GROUP = ("y", "x", "k")
BATCH_GROUP = ("x", "k")
SUM_GROUP = ("zh", "zl")


def head_shard(
    tokens,
    qkv_weight,
    out_weight,
    mask_blocks,
    owner_map,
    pred_stream,
    pred_up,
    pred_down,
    pred_proj,
):
    zh, zl, y, x, k = (lax.axis_index(name) for name in ("zh", "zl", "y", "x", "k"))
    batch = 2 * x + k
    seq = 4 * zh + 2 * zl + y
    place = batch.astype(jnp.int32)[None]
    _, tok_rows, width = tokens.shape
    owners, blk_dev = pred_stream.shape[1], tok_rows // BLK
    pred_width, units = pred_up.shape

    def swap_clips(value):
        return lax.ppermute(value, ("zh", "k"), ((0, 0), (1, 2), (2, 1), (3, 3)))

    def swap(value, bits):
        return lax.ppermute(value, BATCH_GROUP, tuple((i, i ^ bits) for i in range(owners)))

    raw = swap_clips(tokens[0])

    part = width // 8
    stream_blocks = pred_stream[0].reshape(owners, blk_dev, BLK, pred_width)
    owner_here = lax.dynamic_slice_in_dim(owner_map, seq * blk_dev, blk_dev, 1)
    mine = (owner_here == batch)[:, :, None, None]
    compact = jnp.sum(jnp.where(mine, stream_blocks, 0), axis=1).astype(jnp.bfloat16)
    arrived = lax.all_to_all(compact, BATCH_GROUP, split_axis=0, concat_axis=0, tiled=True)

    def chip_columns(which):
        first = which * width + zl * 4 * part + y * part
        pieces = [
            lax.dynamic_slice(
                qkv_weight, (0, first + core * 2 * part), (qkv_weight.shape[0], part)
            )
            for core in range(2)
        ]
        return jnp.concatenate(pieces, axis=1)

    early, *late = (chip_columns(which) for which in range(3))
    late = jnp.stack(late)
    early_two = swap(early, 2)

    raw = after(raw, (arrived, early_two))
    raw_f = raw.astype(jnp.float32)
    normed = layer_norm(raw_f)[0].astype(jnp.bfloat16)
    normed_all = lax.all_gather(normed, CLIP_GROUP, axis=0, tiled=True)
    late_two = swap(late, 2)
    early_one, late_one = swap(early, 1), swap(late, 1)
    early_three = swap(early_two, 1)

    from_owner = take(owner_here, batch)[:, None] == jnp.arange(owners, dtype=jnp.int32)
    stream = jnp.sum(jnp.where(from_owner[:, :, None, None], arrived, 0), axis=1)
    stream = stream.astype(jnp.bfloat16).reshape(tok_rows, pred_width)
    stream = swap_clips(stream)
    normed_pred = layer_norm(stream.astype(jnp.float32))[0].astype(jnp.bfloat16)
    normed_x = swap(normed_pred, 2)
    out_two = swap(after(out_weight, (late_two, normed_x)), 2)

    mine_units = (4 * y + batch).astype(jnp.int32)[None]
    mixed_norm, rstd, up_mine, down_mine = in_vmem(
        forward_kernel,
        (
            jax.ShapeDtypeStruct((tok_rows, pred_width), jnp.float32),
            jax.ShapeDtypeStruct((tok_rows, 1), jnp.float32),
            jax.ShapeDtypeStruct((pred_width, units // 8), jnp.bfloat16),
            jax.ShapeDtypeStruct((4, units // 32, pred_width), jnp.bfloat16),
        ),
        (mine_units, pred_up, pred_down, stream, normed_pred),
        places=1,
        copied=2,
        scratch=(
            pltpu.VMEM(pred_up.shape, jnp.bfloat16),
            pltpu.VMEM(pred_down.shape, jnp.bfloat16),
            pltpu.SemaphoreType.DMA((2,)),
        ),
    )
    down_mine = down_mine.reshape(units // 8, pred_width)

    late_two = after(late_two, (mixed_norm, normed_x))
    late_three = swap(late_two, 1)

    slab = qkv_weight.shape[0]
    qkv_columns = in_vmem(
        weight_kernel,
        jax.ShapeDtypeStruct((3 * part, width), jnp.bfloat16),
        (
            place,
            k.astype(jnp.int32)[None],
            early,
            late,
            early_one,
            late_one,
            early_two,
            late_two,
            early_three,
            late_three,
        ),
        places=2,
        scratch=(
            pltpu.VMEM((3, owners, slab, 2 * part), jnp.bfloat16),
            pltpu.VMEM((2 * part, width), jnp.bfloat16),
        ),
    )

    clip = 2 * x + zh
    shard = 4 * k + 2 * zl + y
    block_ids = shard * blk_dev + jnp.arange(blk_dev, dtype=jnp.int32)
    masked = jnp.any(take(mask_blocks, clip)[:, None] == block_ids[None, :], axis=0)
    divisor = float(owners * mask_blocks.shape[1])
    live = jnp.repeat(masked.astype(jnp.float32) / divisor, BLK)[:, None]

    normed_all = after(normed_all, (qkv_columns, mixed_norm))
    attended = in_vmem(
        attend_kernel,
        jax.ShapeDtypeStruct((4, 2, part, tok_rows), jnp.bfloat16),
        (qkv_columns, normed_all),
        scratch=(pltpu.VMEM((3 * part, normed_all.shape[0]), jnp.float32),),
    )
    pair = jnp.stack([normed_pred, normed_x])
    quad = jnp.concatenate([pair, lax.ppermute(pair, "y", ((0, 1), (1, 0)))])
    quad_core = swap(quad, 1)
    attended = lax.all_to_all(attended, CHIP_GROUP, split_axis=0, concat_axis=0, tiled=True)
    attended = after(attended, quad_core)
    keep, give = in_vmem(
        partial_kernel,
        [jax.ShapeDtypeStruct((tok_rows, width), dtype) for dtype in (jnp.float32, jnp.bfloat16)],
        (
            x.astype(jnp.int32)[None],
            k.astype(jnp.int32)[None],
            out_weight,
            out_two,
            attended,
        ),
        places=2,
        copied=2,
        scratch=(
            pltpu.VMEM((2, slab, width), jnp.bfloat16),
            pltpu.SemaphoreType.DMA((2,)),
        ),
    )
    got = swap(give, 1)
    grad_mixed = in_vmem(
        loss_kernel,
        jax.ShapeDtypeStruct((tok_rows, pred_width), jnp.bfloat16),
        (raw, keep, got, mixed_norm, rstd, live, pred_proj),
    )
    grad_rows = lax.all_gather(grad_mixed, ROW_GROUP, axis=0, tiled=True)
    grads = in_vmem(
        grads_kernel,
        jax.ShapeDtypeStruct((4, units // 16, pred_width), jnp.bfloat16),
        (
            mine_units,
            grad_rows.reshape(8, tok_rows, pred_width),
            quad,
            quad_core,
            up_mine,
            down_mine,
        ),
        places=1,
        scratch=(pltpu.VMEM((8, tok_rows, pred_width), jnp.bfloat16),) * 2,
    )
    grads = lax.all_to_all(grads, SUM_GROUP, split_axis=0, concat_axis=0, tiled=True)
    total = jnp.sum(grads.astype(jnp.float32), axis=0)
    half = units // 32
    return total[:half].T, total[half:]


def solution(mesh):
    if mesh.shape["seq"] == 8 and mesh.shape["batch"] == 4:
        names = ("zh", "zl", "y", "x", "k")
        step, batch, seq = head_shard, BATCH_GROUP, names[:3]
        mesh = jax.sharding.Mesh(mesh.devices.reshape(2, 2, 2, 2, 2), names)
    else:
        step, batch, seq = per_device, "batch", "seq"
    everyone = (seq, batch) if isinstance(seq, str) else seq + batch
    in_specs = (
        P(batch, seq, None),
        P(batch, None),
        P(batch, None),
        P(),
        P(),
        P(batch, None, seq, None),
        P(),
        P(),
        P(),
    )
    out_specs = (P(None, everyone), P(everyone, None))
    return jax.shard_map(step, mesh=mesh, in_specs=in_specs, out_specs=out_specs, check_vma=False)
```

```python
import jax
import jax.numpy as jnp
from jax import lax
from jax.experimental import pallas as pl
from jax.experimental.pallas import tpu as pltpu
from jax.sharding import PartitionSpec as P

H = 16
HD = 88
BLK = 64


gelu_coef = 0.7978845608
gelu_cube = 0.044715


def layer_norm(values):
    center = values - jnp.mean(values, axis=-1, keepdims=True)
    variance = jnp.mean(center * center, axis=-1, keepdims=True)
    factor = lax.rsqrt(variance + 1e-06)
    return (center * factor, factor)


def gelu_tanh(values):
    inner = gelu_coef * (values + gelu_cube * values * values * values)
    return 0.5 * values * (1.0 + jnp.tanh(inner))


def gelu_slope(values):
    inner = gelu_coef * (values + gelu_cube * values * values * values)
    tangent = jnp.tanh(inner)
    return 0.5 * (1.0 + tangent) + 0.5 * values * (1.0 - tangent * tangent) * gelu_coef * (
        1.0 + 3.0 * gelu_cube * values * values
    )


def predictor_grads(stream, target_rows, live_rows, pred_up, pred_down, pred_proj, divisor):
    stream_f = stream.astype(jnp.float32)
    normed_pred = layer_norm(stream_f)[0].astype(jnp.bfloat16)
    hidden_pre = jnp.dot(normed_pred, pred_up, preferred_element_type=jnp.float32)
    hidden = gelu_tanh(hidden_pre).astype(jnp.bfloat16)
    mixed = stream_f + jnp.dot(hidden, pred_down, preferred_element_type=jnp.float32)
    mixed_norm, rstd = layer_norm(mixed)
    mixed_rounded = mixed_norm.astype(jnp.bfloat16)
    prediction = jnp.dot(mixed_rounded, pred_proj, preferred_element_type=jnp.float32)
    error = (prediction - target_rows.astype(jnp.float32)) * live_rows[:, None]
    grad_pred = (error / divisor).astype(jnp.bfloat16)
    grad_norm = jnp.dot(grad_pred, pred_proj.T, preferred_element_type=jnp.float32)
    first_mean = jnp.mean(grad_norm, axis=-1, keepdims=True)
    second_mean = jnp.mean(grad_norm * mixed_norm, axis=-1, keepdims=True)
    grad_mixed = (rstd * (grad_norm - first_mean - mixed_norm * second_mean)).astype(jnp.bfloat16)
    grad_down = jnp.dot(hidden.T, grad_mixed, preferred_element_type=jnp.float32)
    grad_hidden = jnp.dot(grad_mixed, pred_down.T, preferred_element_type=jnp.float32)
    grad_pre = (grad_hidden * gelu_slope(hidden_pre)).astype(jnp.bfloat16)
    grad_up = jnp.dot(normed_pred.T, grad_pre, preferred_element_type=jnp.float32)
    return (grad_up, grad_down)


def per_device(
    tokens,
    qkv_weight,
    out_weight,
    mask_blocks,
    owner_map,
    pred_stream,
    pred_up,
    pred_down,
    pred_proj,
):
    stream_in = tokens[0]
    tok_rows, width = stream_in.shape
    clip_now = lax.axis_index("batch")
    shard_now = lax.axis_index("seq")
    owners = lax.axis_size("batch")
    stream_f = stream_in.astype(jnp.float32)
    normed = layer_norm(stream_f)[0].astype(jnp.bfloat16)

    def fold_rows(left, piece):
        return jnp.dot(left, piece, preferred_element_type=jnp.float32)

    projected = fold_rows(normed, lax.all_gather(qkv_weight, "batch", axis=0, tiled=True))
    projected = projected.astype(jnp.bfloat16)
    queries = projected[:, :width].reshape(tok_rows, H, HD)
    keys_values = projected[:, width:]
    scale = 1.0 / HD**0.5

    def attend_block(carry, block):
        weighted, totals = carry
        block_keys = block[:, :width].reshape(block.shape[0], H, HD)
        block_values = block[:, width:].reshape(block.shape[0], H, HD)
        scores = (
            jnp.einsum("qhd,khd->hqk", queries, block_keys, preferred_element_type=jnp.float32)
            * scale
        )
        weights = jnp.exp(scores)
        totals = totals + jnp.sum(weights, axis=2)
        weighted = weighted + jnp.einsum(
            "hqk,khd->qhd",
            weights.astype(jnp.bfloat16),
            block_values,
            preferred_element_type=jnp.float32,
        )
        return (weighted, totals)

    start_state = (jnp.zeros((tok_rows, H, HD), jnp.float32), jnp.zeros((H, tok_rows), jnp.float32))
    piece = lax.all_gather(keys_values, "seq", axis=0, tiled=True)
    rows = piece.shape[0]
    blocks = piece.reshape(rows // 512, 512, piece.shape[1])
    weighted, totals = lax.scan(
        lambda state, block: (attend_block(state, block), None), start_state, blocks
    )[0]
    attended = (weighted / totals.T[:, :, None]).reshape(tok_rows, width).astype(jnp.bfloat16)
    attn_out = fold_rows(attended, lax.all_gather(out_weight, "batch", axis=0, tiled=True))
    target = layer_norm(stream_f + attn_out)[0].astype(jnp.bfloat16)
    blocks_dev = tok_rows // BLK
    block_ids = shard_now * blocks_dev + jnp.arange(blocks_dev, dtype=jnp.int32)
    owner_ids = jnp.arange(owners, dtype=jnp.int32)
    all_masked = jnp.any(mask_blocks[:, :, None] == block_ids[None, None, :], axis=1)
    all_owner = lax.dynamic_slice_in_dim(owner_map, shard_now * blocks_dev, blocks_dev, 1)
    my_masked = lax.dynamic_slice_in_dim(all_masked, clip_now, 1, 0)[0]
    my_owner = lax.dynamic_slice_in_dim(all_owner, clip_now, 1, 0)[0]
    send_select = (my_masked[None, :] & (my_owner[None, :] == owner_ids[:, None])).astype(
        jnp.bfloat16
    )
    target_blocks = target.reshape(blocks_dev, BLK, width)
    outgoing = jnp.einsum(
        "ob,brd->ord", send_select, target_blocks, preferred_element_type=jnp.float32
    ).astype(jnp.bfloat16)
    incoming = lax.all_to_all(outgoing, "batch", split_axis=0, concat_axis=0, tiled=True)
    recv_flags = all_masked & (all_owner == clip_now)
    recv_select = recv_flags.astype(jnp.bfloat16)
    live_clip = jnp.any(recv_flags, axis=1).astype(jnp.float32)
    live_rows = jnp.broadcast_to(live_clip[:, None], (owners, BLK)).reshape(owners * BLK)
    stream_blocks = pred_stream[0].reshape(owners, blocks_dev, BLK, pred_stream.shape[3])
    stream_picked = jnp.einsum(
        "cb,cbrd->crd", recv_select, stream_blocks, preferred_element_type=jnp.float32
    ).astype(jnp.bfloat16)
    stream_rows = stream_picked.reshape(owners * BLK, pred_stream.shape[3])
    target_rows = incoming.reshape(owners * BLK, width)
    divisor = float(owners * mask_blocks.shape[1])
    grad_up, grad_down = predictor_grads(
        stream_rows, target_rows, live_rows, pred_up, pred_down, pred_proj, divisor
    )
    return (
        lax.psum_scatter(grad_up, ("seq", "batch"), scatter_dimension=1, tiled=True),
        lax.psum_scatter(grad_down, ("seq", "batch"), scatter_dimension=0, tiled=True),
    )


def after(value, other):
    return lax.optimization_barrier((value, other))[0]


def take(array, index):
    return lax.dynamic_index_in_dim(array, index, 0, keepdims=False)


def start_copies(pairs, sems):
    copies = [pltpu.make_async_copy(*pair, sems.at[i]) for i, pair in enumerate(pairs)]
    for copy in copies:
        copy.start()
    return copies


def weight_kernel(place_ref, core_ref, *refs):
    *piece_refs, out_ref, held, turned = refs
    place, core = place_ref[0], core_ref[0]
    parts, slabs, rows, columns = held.shape
    part = out_ref.shape[0] // parts
    for step in range(slabs):
        held[0, place ^ step] = piece_refs[2 * step][...]
        held[1:, place ^ step] = piece_refs[2 * step + 1][...]
    for which in range(parts):
        turned[...] = held[which].reshape(slabs * rows, columns).T
        start = pl.multiple_of(core * part, part)
        out_ref[which * part : (which + 1) * part, :] = turned[pl.ds(start, part), :]


def attend_kernel(weight_ref, normed_ref, out_ref, projected):
    projected[...] = lax.dot_general(
        weight_ref[...],
        normed_ref[...],
        (((1,), (1,)), ((), ())),
        preferred_element_type=jnp.float32,
    )
    part = projected.shape[0] // 3
    chips, cores, _, block_rows = out_ref.shape
    pad = jnp.zeros((-HD % 128, projected.shape[1]), jnp.float32)
    log2_scale = 1.4426950408889634 / HD**0.5

    def head_rows(which, head):
        start = which * part + head * HD
        rows = projected[start : start + HD, :]
        return jnp.concatenate([rows, pad], axis=0).astype(jnp.bfloat16)

    heads = part // HD
    operands = [(head_rows(0, h), head_rows(1, h).T, head_rows(2, h)) for h in range(heads)]
    span = block_rows * cores
    for chip in range(chips):
        joined = []
        for queries, keys, values in operands:
            scores = jnp.dot(
                keys,
                queries[:, chip * span : (chip + 1) * span],
                preferred_element_type=jnp.float32,
            )
            weights = jnp.exp2(scores * log2_scale)
            totals = jnp.sum(weights, axis=0, keepdims=True)
            summed = jnp.dot(
                values, weights.astype(jnp.bfloat16), preferred_element_type=jnp.float32
            )
            joined.append(summed[:HD] / totals)
        attended = jnp.concatenate(joined, axis=0).astype(jnp.bfloat16)
        for core in range(cores):
            out_ref[chip, core] = attended[:, core * block_rows : (core + 1) * block_rows]


def partial_kernel(
    x_ref, core_ref, two_ref, own_ref, att_ref, keep_ref, give_ref
):
    x, core = x_ref[0], core_ref[0]
    sums = [0.0, 0.0]
    for step, slab_ref in enumerate((own_ref, two_ref)):
        place = 2 * (x ^ step)
        for side in range(2):
            rows = [att_ref[place + piece, core ^ side] for piece in range(2)]
            sums[side] = sums[side] + lax.dot_general(
                jnp.concatenate(rows, axis=0),
                slab_ref[...],
                (((0,), (0,)), ((), ())),
                preferred_element_type=jnp.float32,
            )
    keep_ref[...], give_ref[...] = sums[0], sums[1].astype(give_ref.dtype)


def loss_kernel(
    raw_ref, keep_ref, got_ref, mixed_norm_ref, rstd_ref, live_ref, proj_ref, out_ref
):
    mixed_norm = mixed_norm_ref[...]
    prediction = jnp.dot(
        mixed_norm.astype(jnp.bfloat16), proj_ref[...], preferred_element_type=jnp.float32
    )
    summed = raw_ref[...].astype(jnp.float32) + (keep_ref[...] + got_ref[...].astype(jnp.float32))
    target = layer_norm(summed)[0].astype(jnp.bfloat16)
    error = (prediction - target.astype(jnp.float32)) * live_ref[...]
    grad_pred = error.astype(jnp.bfloat16)
    grad_norm = lax.dot_general(
        grad_pred, proj_ref[...], (((1,), (1,)), ((), ())), preferred_element_type=jnp.float32
    )
    first_mean = jnp.mean(grad_norm, axis=-1, keepdims=True)
    second_mean = jnp.mean(grad_norm * mixed_norm, axis=-1, keepdims=True)
    out_ref[...] = (rstd_ref[...] * (grad_norm - first_mean - mixed_norm * second_mean)).astype(
        jnp.bfloat16
    )


def forward_kernel(
    mine_ref,
    up_hbm,
    down_hbm,
    stream_ref,
    normed_ref,
    mixed_norm_ref,
    rstd_ref,
    up_mine_ref,
    down_mine_ref,
    up_ref,
    down_ref,
    sems,
):
    copies = start_copies([(up_hbm, up_ref), (down_hbm, down_ref)], sems)
    copies[0].wait()
    hidden = gelu_tanh(
        jnp.dot(normed_ref[...], up_ref[...], preferred_element_type=jnp.float32)
    ).astype(jnp.bfloat16)
    copies[1].wait()
    mixed = stream_ref[...].astype(jnp.float32) + jnp.dot(
        hidden, down_ref[...], preferred_element_type=jnp.float32
    )
    mixed_norm, rstd = layer_norm(mixed)
    mixed_norm_ref[...] = mixed_norm
    rstd_ref[...] = rstd
    mine = mine_ref[0]
    pieces, share, _ = down_mine_ref.shape
    span = up_ref.shape[1] // pieces
    row = lax.broadcasted_iota(jnp.int32, (span, share), 0)
    column = lax.broadcasted_iota(jnp.int32, (span, share), 1)
    pick = (row == column + mine * share).astype(jnp.float32).astype(jnp.bfloat16)
    picked = []
    for piece in range(pieces):
        window = up_ref[:, piece * span : (piece + 1) * span]
        picked.append(jnp.dot(window, pick, preferred_element_type=jnp.float32))
        start = pl.multiple_of(piece * span + mine * share, 16)
        down_mine_ref[piece] = down_ref[pl.ds(start, share), :]
    up_mine_ref[...] = jnp.concatenate(picked, axis=1).astype(jnp.bfloat16)


def grads_kernel(
    mine_ref, grad_ref, quad_ref, quad_core_ref, up_ref, down_ref, out_ref, grads, normed_rows
):
    mine = mine_ref[0]
    for core, half_ref in enumerate((quad_ref, quad_core_ref)):
        normed_rows[4 * core : 4 * core + 4] = half_ref[...]
        for piece in range(4):
            grads[4 * core + piece] = grad_ref[mine ^ (2 * piece + core)]
    rows = grads.shape[0] * grads.shape[1]
    grad_mixed = grads[...].reshape(rows, grads.shape[2])
    normed = normed_rows[...].reshape(rows, grads.shape[2])
    pre = jnp.dot(normed, up_ref[...], preferred_element_type=jnp.float32)
    hidden = gelu_tanh(pre).astype(jnp.bfloat16)
    pieces, half, _ = out_ref.shape
    half = half // 2
    over_rows = (((0,), (0,)), ((), ()))
    grad_down = lax.dot_general(
        hidden, grad_mixed, over_rows, preferred_element_type=jnp.float32
    )
    grad_hidden = lax.dot_general(
        grad_mixed, down_ref[...], (((1,), (1,)), ((), ())), preferred_element_type=jnp.float32
    )
    grad_pre = (grad_hidden * gelu_slope(pre)).astype(jnp.bfloat16)
    grad_up = lax.dot_general(grad_pre, normed, over_rows, preferred_element_type=jnp.float32)
    for piece in range(pieces):
        rows = slice(piece * half, (piece + 1) * half)
        out_ref[piece, :half, :] = grad_up[rows].astype(jnp.bfloat16)
        out_ref[piece, half:, :] = grad_down[rows].astype(jnp.bfloat16)


def in_vmem(kernel, out_shape, operands, places=0, scratch=(), mib=32, copied=0):
    several = isinstance(out_shape, (list, tuple))
    in_place = pl.BlockSpec(memory_space=pltpu.VMEM)
    return pl.pallas_call(
        kernel,
        out_shape=out_shape,
        in_specs=[pl.BlockSpec(memory_space=pltpu.SMEM)] * places
        + [pl.BlockSpec(memory_space=pltpu.HBM)] * copied
        + [in_place] * (len(operands) - places - copied),
        out_specs=[in_place] * len(out_shape) if several else in_place,
        scratch_shapes=list(scratch),
        cost_estimate=pl.CostEstimate(flops=1, bytes_accessed=1, transcendentals=0),
        compiler_params=pltpu.CompilerParams(vmem_limit_bytes=mib * 2**20),
    )(*operands)


CLIP_GROUP = ("zl", "y", "k")
CHIP_GROUP = ("zl", "y")
ROW_GROUP = ("y", "x", "k")
BATCH_GROUP = ("x", "k")
SUM_GROUP = ("zh", "zl")


def head_shard(
    tokens,
    qkv_weight,
    out_weight,
    mask_blocks,
    owner_map,
    pred_stream,
    pred_up,
    pred_down,
    pred_proj,
):
    zh, zl, y, x, k = (lax.axis_index(name) for name in ("zh", "zl", "y", "x", "k"))
    batch = 2 * x + k
    seq = 4 * zh + 2 * zl + y
    place = batch.astype(jnp.int32)[None]
    _, tok_rows, width = tokens.shape
    owners, blk_dev = pred_stream.shape[1], tok_rows // BLK
    pred_width, units = pred_up.shape

    def swap_clips(value):
        return lax.ppermute(value, ("zh", "k"), ((0, 0), (1, 2), (2, 1), (3, 3)))

    def swap(value, bits):
        return lax.ppermute(value, BATCH_GROUP, tuple((i, i ^ bits) for i in range(owners)))

    raw = swap_clips(tokens[0])

    part = width // 8
    stream_blocks = pred_stream[0].reshape(owners, blk_dev, BLK, pred_width)
    owner_here = lax.dynamic_slice_in_dim(owner_map, seq * blk_dev, blk_dev, 1)
    mine = (owner_here == batch)[:, :, None, None]
    compact = jnp.sum(jnp.where(mine, stream_blocks, 0), axis=1).astype(jnp.bfloat16)
    arrived = lax.all_to_all(compact, BATCH_GROUP, split_axis=0, concat_axis=0, tiled=True)

    def chip_columns(which):
        first = which * width + zl * 4 * part + y * part
        pieces = [
            lax.dynamic_slice(
                qkv_weight, (0, first + core * 2 * part), (qkv_weight.shape[0], part)
            )
            for core in range(2)
        ]
        return jnp.concatenate(pieces, axis=1)

    early, *late = (chip_columns(which) for which in range(3))
    late = jnp.stack(late)
    early_two = swap(early, 2)

    raw = after(raw, (arrived, early_two))
    raw_f = raw.astype(jnp.float32)
    normed = layer_norm(raw_f)[0].astype(jnp.bfloat16)
    normed_all = lax.all_gather(normed, CLIP_GROUP, axis=0, tiled=True)
    late_two = swap(late, 2)
    early_one, late_one = swap(early, 1), swap(late, 1)
    early_three = swap(early_two, 1)

    from_owner = take(owner_here, batch)[:, None] == jnp.arange(owners, dtype=jnp.int32)
    stream = jnp.sum(jnp.where(from_owner[:, :, None, None], arrived, 0), axis=1)
    stream = stream.astype(jnp.bfloat16).reshape(tok_rows, pred_width)
    stream = swap_clips(stream)
    normed_pred = layer_norm(stream.astype(jnp.float32))[0].astype(jnp.bfloat16)
    normed_x = swap(normed_pred, 2)
    out_two = swap(after(out_weight, (late_two, normed_x)), 2)

    mine_units = (4 * y + batch).astype(jnp.int32)[None]
    mixed_norm, rstd, up_mine, down_mine = in_vmem(
        forward_kernel,
        (
            jax.ShapeDtypeStruct((tok_rows, pred_width), jnp.float32),
            jax.ShapeDtypeStruct((tok_rows, 1), jnp.float32),
            jax.ShapeDtypeStruct((pred_width, units // 8), jnp.bfloat16),
            jax.ShapeDtypeStruct((4, units // 32, pred_width), jnp.bfloat16),
        ),
        (mine_units, pred_up, pred_down, stream, normed_pred),
        places=1,
        copied=2,
        scratch=(
            pltpu.VMEM(pred_up.shape, jnp.bfloat16),
            pltpu.VMEM(pred_down.shape, jnp.bfloat16),
            pltpu.SemaphoreType.DMA((2,)),
        ),
    )
    down_mine = down_mine.reshape(units // 8, pred_width)

    late_two = after(late_two, (mixed_norm, normed_x))
    late_three = swap(late_two, 1)

    slab = qkv_weight.shape[0]
    qkv_columns = in_vmem(
        weight_kernel,
        jax.ShapeDtypeStruct((3 * part, width), jnp.bfloat16),
        (
            place,
            k.astype(jnp.int32)[None],
            early,
            late,
            early_one,
            late_one,
            early_two,
            late_two,
            early_three,
            late_three,
        ),
        places=2,
        scratch=(
            pltpu.VMEM((3, owners, slab, 2 * part), jnp.bfloat16),
            pltpu.VMEM((2 * part, width), jnp.bfloat16),
        ),
    )

    clip = 2 * x + zh
    shard = 4 * k + 2 * zl + y
    block_ids = shard * blk_dev + jnp.arange(blk_dev, dtype=jnp.int32)
    masked = jnp.any(take(mask_blocks, clip)[:, None] == block_ids[None, :], axis=0)
    divisor = float(owners * mask_blocks.shape[1])
    live = jnp.repeat(masked.astype(jnp.float32) / divisor, BLK)[:, None]

    normed_all = after(normed_all, (qkv_columns, mixed_norm))
    attended = in_vmem(
        attend_kernel,
        jax.ShapeDtypeStruct((4, 2, part, tok_rows), jnp.bfloat16),
        (qkv_columns, normed_all),
        scratch=(pltpu.VMEM((3 * part, normed_all.shape[0]), jnp.float32),),
    )
    pair = jnp.stack([normed_pred, normed_x])
    quad = jnp.concatenate([pair, lax.ppermute(pair, "y", ((0, 1), (1, 0)))])
    quad_core = swap(quad, 1)
    attended = lax.all_to_all(attended, CHIP_GROUP, split_axis=0, concat_axis=0, tiled=True)
    attended = after(attended, quad_core)
    keep, give = in_vmem(
        partial_kernel,
        [jax.ShapeDtypeStruct((tok_rows, width), dtype) for dtype in (jnp.float32, jnp.bfloat16)],
        (
            x.astype(jnp.int32)[None],
            k.astype(jnp.int32)[None],
            out_two,
            out_weight,
            attended,
        ),
        places=2,
    )
    got = swap(give, 1)
    grad_mixed = in_vmem(
        loss_kernel,
        jax.ShapeDtypeStruct((tok_rows, pred_width), jnp.bfloat16),
        (raw, keep, got, mixed_norm, rstd, live, pred_proj),
    )
    grad_rows = lax.all_gather(grad_mixed, ROW_GROUP, axis=0, tiled=True)
    grads = in_vmem(
        grads_kernel,
        jax.ShapeDtypeStruct((4, units // 16, pred_width), jnp.bfloat16),
        (
            mine_units,
            grad_rows.reshape(8, tok_rows, pred_width),
            quad,
            quad_core,
            up_mine,
            down_mine,
        ),
        places=1,
        scratch=(pltpu.VMEM((8, tok_rows, pred_width), jnp.bfloat16),) * 2,
    )
    grads = lax.all_to_all(grads, SUM_GROUP, split_axis=0, concat_axis=0, tiled=True)
    total = jnp.sum(grads.astype(jnp.float32), axis=0)
    half = units // 32
    return total[:half].T, total[half:]


def solution(mesh):
    if mesh.shape["seq"] == 8 and mesh.shape["batch"] == 4:
        names = ("zh", "zl", "y", "x", "k")
        step, batch, seq = head_shard, BATCH_GROUP, names[:3]
        mesh = jax.sharding.Mesh(mesh.devices.reshape(2, 2, 2, 2, 2), names)
    else:
        step, batch, seq = per_device, "batch", "seq"
    everyone = (seq, batch) if isinstance(seq, str) else seq + batch
    in_specs = (
        P(batch, seq, None),
        P(batch, None),
        P(batch, None),
        P(),
        P(),
        P(batch, None, seq, None),
        P(),
        P(),
        P(),
    )
    out_specs = (P(None, everyone), P(everyone, None))
    return jax.shard_map(step, mesh=mesh, in_specs=in_specs, out_specs=out_specs, check_vma=False)
```
